32 devices in a mesh: lat: 2 (over core), lon: 16 (over z, y, x).
Axes of the slice: x: 2, y: 2, z: 4, core: 2. Of those that a mesh axis runs over, the one named last changes fastest.
Arguments:
- features: bfloat16 [32, 128, 256], P('lat', 'lon'), may hold values from -6 to 6
- cotangent: bfloat16 [32, 128, 256], P('lat', 'lon'), may hold values from -6 to 6
- weights: bfloat16 [8, 256, 256], replicated, may hold values from -0.375 to 0.375
- basis: bfloat16 [8, 32, 3, 5], P(None, 'lat'), may hold values from -1.5 to 1.5
- polar_kernel: float32 [8, 2, 2, 2, 128], replicated, may hold values from -0.375 to 0.375
- lon_reach: int32 [32], P('lat'), may hold values from 0 to 2
Outputs:
- grad_features: bfloat16 [32, 128, 256], P('lat', 'lon')
- grad_weights: float32 [8, 256, 256], P('lat')
The draws below stay inside these ranges and needn't reach their ends.
All inputs are finite; a program needn't handle non-finite values.
Results may differ from the reference program's by a relative error of at most 0.0049.
Values may be sent and summed in bfloat16 or wider, within the bound.
A program may use at most 64 MiB of HBM per device.

```python
import jax
import jax.numpy as jnp
from jax import lax

CHANNELS = 256
KERNELS = 8
RADIUS = 1
REACH = 2
POLAR = 2
NLAT = 32
NLON = 128


def touch_ends(drawn, stream_key, least, largest):
    spot = [jax.random.randint(jax.random.fold_in(stream_key, axis), (), 0, length) for axis, length in enumerate(drawn.shape)]
    longest = drawn.shape.index(max(drawn.shape))
    neighbour = spot[:longest] + [(spot[longest] + 1) % drawn.shape[longest]] + spot[longest + 1:]
    return drawn.at[tuple(spot)].set(least).at[tuple(neighbour)].set(largest)


def block_scale(rng, extent, pieces, low, high):
    def one(position, blocks):
        heights = jax.random.uniform(jax.random.fold_in(jax.random.fold_in(rng, 6), position), (blocks,), jnp.float32, low / len(pieces), high / len(pieces))
        return jnp.repeat(jnp.exp(heights), extent[position] // blocks).reshape((-1,) + (1,) * (len(extent) - position - 1))

    factor_of = one(*pieces[0])
    for cut in pieces[1:]:
        factor_of = factor_of * one(*cut)
    return factor_of


def noise(own_key, shape, deviation, most, pieces=(), kind=jnp.bfloat16):
    drawn = deviation * jax.random.normal(own_key, shape, jnp.float32)
    if pieces:
        drawn = drawn * block_scale(own_key, shape, pieces, -0.22, 0.18)
    return jnp.clip(drawn, -most, most).astype(kind)


def setup_inputs(seed: int = 0) -> dict:
    arg_keys = jax.random.split(jax.random.key(seed), 7)
    return {
        "features": noise(arg_keys[0], (NLAT, NLON, CHANNELS), 1.0, 6.0, ((0, 2), (1, 16))),
        "cotangent": noise(arg_keys[1], (NLAT, NLON, CHANNELS), 1.0, 6.0, ((0, 2), (1, 16))),
        "weights": noise(arg_keys[2], (KERNELS, CHANNELS, CHANNELS), CHANNELS ** -0.5, 0.375),
        "basis": noise(arg_keys[3], (KERNELS, NLAT, 2 * RADIUS + 1, 2 * REACH + 1), 0.3, 1.5, ((1, 2),)),
        "polar_kernel": noise(arg_keys[4], (KERNELS, 2, POLAR, POLAR, NLON), (POLAR * NLON) ** -0.5, 0.375, (), jnp.float32),
        "lon_reach": touch_ends(jax.random.randint(arg_keys[5], (NLAT,), 0, REACH + 1), jax.random.fold_in(arg_keys[5], 1), 0, REACH).astype(jnp.int32),
    }


def pole_pad(values_in):
    half_turn = NLON // 2
    top_rows = jnp.roll(values_in[:RADIUS], -half_turn, axis=1)[::-1]
    bottom_rows = jnp.roll(values_in[NLAT - RADIUS:], -half_turn, axis=1)[::-1]
    lengthened = jnp.concatenate([top_rows, values_in, bottom_rows], axis=0)
    return jnp.concatenate([lengthened[:, NLON - REACH:], lengthened, lengthened[:, :REACH]], axis=1)

def zonal(rows_in, kernel):
    spectrum = jnp.fft.rfft(rows_in, axis=1)
    kernel_spec = jnp.conj(jnp.fft.rfft(kernel, axis=2))
    product = jnp.einsum('abm,bmc->amc', kernel_spec, spectrum)
    return jnp.fft.irfft(product, n=NLON, axis=1)

def basis_map(values_in, masked_k, kernel_k):
    widened = pole_pad(values_in)
    summed = jnp.zeros_like(values_in)
    for row_off in range(2 * RADIUS + 1):
        for col_off in range(2 * REACH + 1):
            summed = summed + masked_k[:, row_off, col_off][:, None, None] * widened[row_off:row_off + NLAT, col_off:col_off + NLON]
    north_part = zonal(values_in[:POLAR], kernel_k[0])
    south_part = zonal(values_in[NLAT - POLAR:], kernel_k[1])
    summed = summed.at[:POLAR].add(north_part)
    return summed.at[NLAT - POLAR:].add(south_part)

def reference(features, cotangent, weights, basis, polar_kernel, lon_reach):
    offsets = jnp.abs(jnp.arange(2 * REACH + 1, dtype=jnp.int32) - REACH)
    reach_mask = (offsets[None, :] <= lon_reach[:, None]).astype(jnp.float32)
    masked = basis.astype(jnp.float32) * reach_mask[None, :, None, :]
    values_f = features.astype(jnp.float32)
    cotangent_f = cotangent.astype(jnp.float32)

    def per_kernel(grad_acc, inputs):
        masked_k, kernel_k, weight_k = inputs
        basis_out, pullback = jax.vjp(lambda values_in: basis_map(values_in, masked_k, kernel_k), values_f)
        rounded = lax.optimization_barrier(basis_out.astype(jnp.bfloat16)).astype(jnp.float32)
        grad_w = jnp.einsum('ijc,ijo->co', rounded, cotangent_f)
        grad_basis = jnp.einsum('ijo,co->ijc', cotangent_f, weight_k.astype(jnp.float32))
        grad_basis = lax.optimization_barrier(grad_basis.astype(jnp.bfloat16)).astype(jnp.float32)
        grad_back, = pullback(grad_basis)
        return (grad_acc + grad_back, grad_w)
    grad_acc, grad_weights = lax.scan(per_kernel, jnp.zeros_like(values_f), (masked, polar_kernel, weights))
    return (grad_acc.astype(jnp.bfloat16), grad_weights)
```

```python
import functools

import jax
import jax.numpy as jnp
import numpy as np
from jax import lax
from jax.experimental import pallas as pl
from jax.experimental.pallas import tpu as pltpu
from jax.sharding import PartitionSpec as P

RADIUS = 1
REACH = 2
POLAR = 2


def padded(cells, sides, width, closed):
    for axis, dim in sides:
        count = lax.axis_size(axis)
        ends = count if closed else count - 1
        head = lax.slice_in_dim(cells, 0, width, axis=dim)
        tail = lax.slice_in_dim(cells, cells.shape[dim] - width, cells.shape[dim], axis=dim)
        cells = jnp.concatenate(
            [
                lax.ppermute(tail, axis, [(i, (i + 1) % count) for i in range(ends)]),
                cells,
                lax.ppermute(head, axis, [((i + 1) % count, i) for i in range(ends)]),
            ],
            axis=dim,
        )
    return cells


def from_behind(block, axis, distance):
    devices = range(lax.axis_size(axis))
    route = [((i - distance) % len(devices), i) for i in devices]
    return lax.ppermute(block, axis, route)


def on_device(features, cotangent, weights, basis, polar_kernel, lon_reach):
    lat_rows, lon_cols, channels = features.shape
    kernels = weights.shape[0]
    lat_count = lax.axis_size("lat")
    lon_count = lax.axis_size("lon")
    lat_index = lax.axis_index("lat")
    lon_index = lax.axis_index("lon")
    at_north = lat_index == 0
    at_south = lat_index == lat_count - 1
    at_pole = jnp.logical_or(at_north, at_south)
    lon_total = lon_cols * lon_count
    own_cols = lon_index * lon_cols + jnp.arange(lon_cols, dtype=jnp.int32)
    offsets = jnp.abs(jnp.arange(2 * REACH + 1, dtype=jnp.int32) - REACH)
    reach_mask = (offsets[None, :] <= lon_reach[:, None]).astype(basis.dtype)
    masked = basis * reach_mask[None, :, None, :]
    neighbours = padded(features, (("lat", 0),), RADIUS, False)
    partner_rows = from_behind(
        (features[:RADIUS], features[lat_rows - RADIUS :]), "lon", lon_count // 2
    )
    upper_rows = jnp.where(at_north, partner_rows[0][::-1], neighbours[:RADIUS])
    lower_rows = jnp.where(at_south, partner_rows[1][::-1], neighbours[lat_rows + RADIUS :])
    lengthened = jnp.concatenate([upper_rows, features, lower_rows], 0)
    widened = padded(lengthened, (("lon", 1),), REACH, True)
    basis_sum = jnp.zeros((kernels, lat_rows, lon_cols, channels), jnp.float32)
    for row_off in range(2 * RADIUS + 1):
        windows = jnp.stack(
            [
                widened[row_off : row_off + lat_rows, col_off : col_off + lon_cols]
                for col_off in range(2 * REACH + 1)
            ],
            1,
        )
        basis_sum = basis_sum + jnp.einsum(
            "kib,ibjc->kijc", masked[:, :, row_off], windows, preferred_element_type=jnp.float32
        )
    hemisphere = jnp.where(at_north, polar_kernel[:, 0], polar_kernel[:, 1])
    polar_in = jnp.where(at_north, features[:POLAR], features[lat_rows - POLAR :])
    polar_zero = jnp.zeros((kernels, POLAR, lon_cols, channels), jnp.float32)
    block_rows = lax.all_gather(polar_in, "lon", axis=1, tiled=True)

    def compute():
        source = jnp.arange(block_rows.shape[1], dtype=jnp.int32)
        offset_idx = (source[:, None] - own_cols[None, :]) % lon_total
        circulant = jnp.take(hemisphere, offset_idx, axis=3)
        return jnp.einsum(
            "kabuj,buc->kajc",
            circulant,
            block_rows.astype(jnp.float32),
            precision=lax.Precision.HIGHEST,
        )

    polar_out = lax.cond(at_pole, compute, lambda: polar_zero)
    basis_sum = basis_sum.at[:, :POLAR].add(jnp.where(at_north, polar_out, 0.0))
    basis_sum = basis_sum.at[:, lat_rows - POLAR :].add(jnp.where(at_south, polar_out, 0.0))
    contracted = basis_sum.astype(jnp.bfloat16)
    band_grad = lax.psum_scatter(
        jnp.einsum("kijc,ijo->kco", contracted, cotangent, preferred_element_type=jnp.float32),
        "lat",
        scatter_dimension=0,
        tiled=True,
    )
    grad_weights = lax.psum(band_grad, "lon")
    grad_basis = jnp.einsum(
        "kco,ijo->kijc", weights, cotangent, preferred_element_type=jnp.float32
    ).astype(jnp.bfloat16)
    grad_wide = jnp.zeros((lat_rows + 2 * RADIUS, lon_cols + 2 * REACH, channels), jnp.float32)
    for row_off in range(2 * RADIUS + 1):
        grad_win = jnp.einsum(
            "kib,kijc->ibjc", masked[:, :, row_off], grad_basis, preferred_element_type=jnp.float32
        )
        for col_off in range(2 * REACH + 1):
            grad_wide = grad_wide.at[
                row_off : row_off + lat_rows, col_off : col_off + lon_cols
            ].add(grad_win[:, col_off])
    lon_rims = jnp.concatenate([grad_wide[:, :REACH], grad_wide[:, lon_cols + REACH :]], 1)
    beside_all = padded(lon_rims, (("lon", 1),), REACH, True)
    folded = grad_wide[:, REACH : lon_cols + REACH]
    folded = folded.at[:, :REACH].add(beside_all[:, :REACH])
    folded = folded.at[:, lon_cols - REACH :].add(beside_all[:, 3 * REACH :])
    ghosts = jnp.concatenate([folded[:RADIUS], folded[lat_rows + RADIUS :]], 0)
    beside = padded(ghosts, (("lat", 0),), RADIUS, False)
    turned = from_behind((folded[:RADIUS], folded[lat_rows + RADIUS :]), "lon", lon_count // 2)
    interior = folded[RADIUS : lat_rows + RADIUS]
    from_above = jnp.where(at_north, turned[0][::-1], beside[:RADIUS])
    from_below = jnp.where(at_south, turned[1][::-1], beside[3 * RADIUS :])
    interior = interior.at[:RADIUS].add(from_above)
    interior = interior.at[lat_rows - RADIUS :].add(from_below)
    polar_cot = jnp.where(at_north, cotangent[:POLAR], cotangent[lat_rows - POLAR :])
    running = jnp.zeros((POLAR, lon_cols, channels), jnp.float32)
    add_block_rows = lax.all_gather(polar_cot, "lon", axis=1, tiled=True)

    def compute():
        source = jnp.arange(add_block_rows.shape[1], dtype=jnp.int32)
        offset_idx = (own_cols[None, :] - source[:, None]) % lon_total
        circulant = jnp.take(hemisphere, offset_idx, axis=3)
        block_grad = jnp.einsum(
            "kco,auo->kauc", weights, add_block_rows, preferred_element_type=jnp.float32
        ).astype(jnp.bfloat16)
        return jnp.einsum(
            "kabuj,kauc->bjc",
            circulant,
            block_grad.astype(jnp.float32),
            precision=lax.Precision.HIGHEST,
        )

    polar_grad = lax.cond(at_pole, compute, lambda: running)
    interior = interior.at[:POLAR].add(jnp.where(at_north, polar_grad, 0.0))
    interior = interior.at[lat_rows - POLAR :].add(jnp.where(at_south, polar_grad, 0.0))
    return (interior.astype(jnp.bfloat16), grad_weights)


COLS = 8
SLOTS = 32
MESH = pl.DeviceIdType.MESH


def spread_matrices():
    taps = 2 * REACH + 1
    forward = np.zeros((2, 3, taps, 2, COLS, 4, SLOTS), np.float32)
    backward = np.zeros((4, 3, taps, 2, COLS, 4, SLOTS), np.float32)
    for inner in range(2):
        for col in range(COLS):
            for row in range(4):
                for slot in range(SLOTS):
                    a, b = row - inner, slot - COLS - col + REACH
                    if 0 <= a < 3 and 0 <= b < taps:
                        forward[inner, a, b, inner, col, row, slot] = 1
                    a, b = inner - row + 2, col + REACH - (slot - COLS)
                    if 0 <= a < 3 and 0 <= b < taps:
                        backward[row, a, b, inner, col, row, slot] = 1
    return forward.reshape(2 * 3 * taps, -1), backward.reshape(4 * 3 * taps, -1)


def split(values):
    high = values.astype(jnp.bfloat16)
    return high, (values - high.astype(jnp.float32)).astype(jnp.bfloat16)


def mul(a, b, dims=((1,), (0,))):
    return lax.dot_general(a, b, (dims, ((), ())), preferred_element_type=jnp.float32)


def fused(
    n, f_ref, c_ref, w_ref, t1_ref, t2_ref, a_ref, b_ref, gf_ref, gw_ref,
    fc, polar, sides, below, near, ext, sums, own, sib_out, sib_in, part, terms, mine, t2n,
    acc, send_polar, recv_polar, send_misc, recv_misc, send_sib, recv_sib,
    send_rs, recv_rs, send_ag, recv_ag,
):
    f32, bf16 = jnp.float32, jnp.bfloat16
    lat, lon = lax.axis_index("lat"), lax.axis_index("lon")
    points, channels = f_ref.shape
    rows = points // COLS
    pairs = rows // 2
    kernels = w_ref.shape[0]
    half_k = kernels // 2
    chunk = half_k * channels // n
    other = 1 - lat
    north = lat == 0

    def turn(t):
        return lax.rem(lon + t, n)

    barrier = pltpu.get_barrier_semaphore()
    for t in range(1, n):
        pl.semaphore_signal(barrier, inc=1, device_id=(lat, turn(t)), device_id_type=MESH)
    for t in (0, 1, n - 1):
        pl.semaphore_signal(barrier, inc=1, device_id=(other, turn(t)), device_id_type=MESH)
    fc[0] = f_ref[...]
    fc[1] = c_ref[...]
    pl.semaphore_wait(barrier, n + 2)

    def push(src, dst, send, recv, to):
        copy = pltpu.make_async_remote_copy(
            src_ref=src, dst_ref=dst, send_sem=send, recv_sem=recv, device_id=to, device_id_type=MESH
        )
        copy.start()
        return copy

    pole_at = pl.multiple_of(lat * (points - 16), 16)
    edge_at = pl.multiple_of(other * (points - 16), 16)
    edge = fc.at[:, pl.ds(edge_at, 16)]
    first = [
        push(fc, sides.at[0], send_misc.at[0], recv_misc.at[0], (lat, turn(1))),
        push(fc, sides.at[1], send_misc.at[1], recv_misc.at[1], (lat, turn(n - 1))),
        push(edge, below.at[1], send_misc.at[2], recv_misc.at[2], (other, lon)),
        push(edge, below.at[0], send_misc.at[3], recv_misc.at[3], (other, turn(1))),
        push(edge, below.at[2], send_misc.at[4], recv_misc.at[4], (other, turn(n - 1))),
        push(t2_ref.at[pairs], near, send_misc.at[5], recv_misc.at[5], (other, lon)),
    ]
    for t in range(1, n):
        first.append(
            push(
                fc.at[:, pl.ds(pole_at, 16)], polar.at[n - t],
                send_polar.at[t], recv_polar.at[n - t], (lat, turn(t)),
            )
        )
    polar[0] = fc[:, pl.ds(pole_at, 16)]
    for copy in first:
        copy.wait()

    def block3(left, mid, right):
        lead = mid.shape[:-2]
        return jnp.concatenate([left, mid, right, jnp.zeros(lead + (COLS, channels), f32)], -2)

    poles = []
    for field in range(2):
        gathered = polar[:, field].astype(f32).reshape(n, 2, COLS, channels)
        pole_rows = [gathered[:, r].reshape(n * COLS, channels) for r in range(2)]
        poles.append(jnp.concatenate(pole_rows, 0).astype(bf16))
        inside = block3(
            sides[0, field].astype(f32).reshape(rows, COLS, channels),
            fc[field].astype(f32).reshape(rows, COLS, channels),
            sides[1, field].astype(f32).reshape(rows, COLS, channels),
        )
        ext[field, pl.ds(SLOTS, rows * SLOTS)] = inside.reshape(rows * SLOTS, channels).astype(bf16)
        turned = gathered[n // 2 - 1 : n // 2 + 2]
        turned = jnp.where(north, turned[:, 0], turned[:, 1])
        beside = below[:, field].astype(f32).reshape(3, 2, COLS, channels)
        beside = jnp.where(north, beside[:, 0], beside[:, 1])
        zeros = jnp.zeros((COLS, channels), f32)
        top = jnp.where(north, turned, beside).reshape(3 * COLS, channels)
        bottom = jnp.where(north, beside, turned).reshape(3 * COLS, channels)
        ext[field, pl.ds(0, SLOTS)] = jnp.concatenate([top, zeros], 0).astype(bf16)
        ext[field, pl.ds((rows + 1) * SLOTS, SLOTS)] = jnp.concatenate([bottom, zeros], 0).astype(bf16)

    high, low = split(a_ref[...])
    zonal = mul(high, poles[0]) + mul(low, poles[0])
    for p in range(pairs):
        taps = t1_ref[p].reshape(kernels * 16, 4 * SLOTS)
        value = mul(taps, ext[0, pl.ds(2 * p * SLOTS, 4 * SLOTS)])
        if p == 0:
            value = value + jnp.where(north, zonal, 0.0)
        if p == pairs - 1:
            value = value + jnp.where(north, 0.0, zonal)
        sums[:, pl.ds(16 * p, 16)] = value.astype(bf16).reshape(kernels, 16, channels)

    cot = c_ref[...]
    to_sib = []
    for j in range(half_k):
        at = pl.ds(j * channels, channels)
        sib_out[at] = mul(sums[other * half_k + j], cot, ((0,), (0,))).astype(bf16)
        to_sib.append(
            push(sib_out.at[at], sib_in.at[at], send_sib.at[j], recv_sib.at[j], (other, lon))
        )
    for j in range(half_k):
        own[pl.ds(j * channels, channels)] = mul(sums[lat * half_k + j], cot, ((0,), (0,)))
    for j in range(half_k):
        at = pl.ds(j * channels, channels)
        to_sib[j].wait()
        part[at] = (own[at] + sib_in[at].astype(f32)).astype(bf16)
    scatter = []
    for t in range(1, n):
        at = pl.ds(pl.multiple_of(turn(t) * chunk, chunk), chunk)
        scatter.append(
            push(part.at[at], terms.at[t], send_rs.at[t], recv_rs.at[t], (lat, turn(t)))
        )

    edge_pair = (pairs - 1) * (1 - lat)
    t2n[...] = near[...]
    acc[...] = jnp.zeros_like(acc)
    pole_acc = jnp.zeros((16, channels), f32)
    near_acc = jnp.zeros((16, channels), f32)

    def per_kernel(k, carry):
        pole_acc, near_acc = carry
        weight = w_ref[k]
        grad = mul(ext[1], weight, ((1,), (1,))).astype(bf16)
        for p in range(pairs):
            window = grad[2 * p * SLOTS : (2 * p + 4) * SLOTS]
            acc[pl.ds(16 * p, 16)] += mul(t2_ref[p, k], window)
        last = grad[(2 * pairs - 2) * SLOTS : (2 * pairs + 2) * SLOTS]
        near_acc += mul(t2n[k], jnp.where(north, last, grad[: 4 * SLOTS]))
        pole_grad = mul(poles[1], weight, ((1,), (1,))).astype(bf16)
        high, low = split(b_ref[k])
        pole_acc += mul(high, pole_grad) + mul(low, pole_grad)
        return pole_acc, near_acc

    pole_acc, near_acc = lax.fori_loop(0, kernels, per_kernel, (pole_acc, near_acc))
    acc[pl.ds(0, 16)] += jnp.where(north, pole_acc, near_acc)
    acc[pl.ds(points - 16, 16)] += jnp.where(north, near_acc, pole_acc)
    gf_ref[...] = acc[...].astype(bf16)

    here = pl.ds(pl.multiple_of(lon * chunk, chunk), chunk)
    total = part[here].astype(f32)
    for t in range(1, n):
        scatter[t - 1].wait()
        total = total + terms[t].astype(f32)
    mine[...] = total.astype(bf16)
    gw_ref[here] = mine[...]
    gather = []
    for t in range(1, n):
        gather.append(push(mine, gw_ref.at[here], send_ag.at[t], recv_ag.at[t], (lat, turn(t))))
    for copy in gather:
        copy.wait()


def in_kernel(features, cotangent, weights, basis, polar_kernel, lon_reach):
    lat_rows, lon_cols, channels = features.shape
    kernels = weights.shape[0]
    n = lax.axis_size("lon")
    north = lax.axis_index("lat") == 0
    pairs, points = lat_rows // 2, lat_rows * lon_cols
    lon_total = lon_cols * n
    offsets = jnp.abs(jnp.arange(2 * REACH + 1, dtype=jnp.int32) - REACH)
    reach_mask = offsets[None, :] <= lon_reach[:, None]
    masked = jnp.where(reach_mask[None, :, None, :], basis, 0)
    spread, back = spread_matrices()
    by_row = jnp.swapaxes(masked, 0, 1)
    flat = by_row.reshape(pairs, 2, kernels, -1).swapaxes(1, 2).reshape(pairs, kernels, -1)
    t1 = jnp.einsum("pkz,zn->pkn", flat, jnp.asarray(spread, jnp.bfloat16))
    t1 = t1.reshape(pairs, kernels, 16, 4 * SLOTS)
    zero_row = jnp.zeros_like(by_row[:1])
    crossed_top = zero_row.at[0, :, 2].set(by_row[0, :, 0])
    crossed_end = zero_row.at[0, :, 0].set(by_row[-1, :, 2])
    longer = jnp.concatenate(
        [jnp.where(north, crossed_top, 0), by_row, jnp.where(north, 0, crossed_end)], 0
    )
    quad = jnp.stack([longer[q : q + lat_rows - 1 : 2] for q in range(4)], 2)
    gap = jnp.zeros_like(by_row[:3])
    edge = jnp.where(
        north, jnp.concatenate([by_row[-1:], gap], 0), jnp.concatenate([gap, by_row[:1]], 0)
    )
    quad = jnp.concatenate([quad, edge.swapaxes(0, 1)[None]], 0)
    quad = quad.reshape(pairs + 1, kernels, -1)
    t2 = jnp.einsum("pkz,zn->pkn", quad, jnp.asarray(back, jnp.bfloat16))
    t2 = t2.reshape(pairs + 1, kernels, 16, 4 * SLOTS)
    zonal = jnp.where(north, polar_kernel[:, 0], polar_kernel[:, 1])
    twice = jnp.concatenate([zonal, zonal], 3)
    a = jnp.stack(
        [twice[..., lon_total - j : 2 * lon_total - j] for j in range(COLS)], 2
    ).reshape(kernels * 16, 2 * lon_total)
    twice = twice[..., ::-1]
    b = jnp.stack(
        [twice[..., lon_total - 1 - j : 2 * lon_total - 1 - j] for j in range(COLS)], 3
    )
    b = jnp.transpose(b, (0, 2, 3, 1, 4)).reshape(kernels, 16, 2 * lon_total)
    half = kernels * channels // 2
    bf16, f32 = jnp.bfloat16, jnp.float32
    dma = pltpu.SemaphoreType.DMA
    vmem = pl.BlockSpec(memory_space=pltpu.VMEM)
    grad_features, grad_weights = pl.pallas_call(
        functools.partial(fused, n),
        out_shape=(
            jax.ShapeDtypeStruct((points, channels), bf16),
            jax.ShapeDtypeStruct((half, channels), bf16),
        ),
        in_specs=[vmem] * 7,
        out_specs=(vmem, vmem),
        scratch_shapes=[
            pltpu.VMEM((2, points, channels), bf16),
            pltpu.VMEM((n, 2, 16, channels), bf16),
            pltpu.VMEM((2, 2, points, channels), bf16),
            pltpu.VMEM((3, 2, 16, channels), bf16),
            pltpu.VMEM((kernels, 16, 4 * SLOTS), bf16),
            pltpu.VMEM((2, (lat_rows + 2) * SLOTS, channels), bf16),
            pltpu.VMEM((kernels, points, channels), bf16),
            pltpu.VMEM((half, channels), f32),
            pltpu.VMEM((half, channels), bf16),
            pltpu.VMEM((half, channels), bf16),
            pltpu.VMEM((half, channels), bf16),
            pltpu.VMEM((n, half // n, channels), bf16),
            pltpu.VMEM((half // n, channels), bf16),
            pltpu.VMEM((kernels, 16, 4 * SLOTS), bf16),
            pltpu.VMEM((points, channels), f32),
            dma((n,)), dma((n,)), dma((6,)), dma((6,)), dma((4,)), dma((4,)),
            dma((n,)), dma((n,)), dma((n,)), dma((n,)),
        ],
        compiler_params=pltpu.CompilerParams(
            collective_id=0, has_side_effects=True, vmem_limit_bytes=32 * 2**20
        ),
    )(
        features.reshape(points, channels), cotangent.reshape(points, channels),
        weights, t1, t2, a, b,
    )
    return (
        grad_features.reshape(features.shape),
        grad_weights.astype(f32).reshape(kernels // 2, channels, channels),
    )


def choose(features, cotangent, weights, basis, polar_kernel, lon_reach):
    rows, cols, channels = features.shape
    n = lax.axis_size("lon")
    kernels = weights.shape[0]
    fits = (
        lax.axis_size("lat") == 2 and cols == COLS and n % 2 == 0 and n >= 4 and rows % 2 == 0
        and rows >= 4 and kernels == 8 and (kernels // 2 * channels) % (16 * n) == 0
    )
    plan = in_kernel if fits else on_device
    return plan(features, cotangent, weights, basis, polar_kernel, lon_reach)


def solution(mesh):
    in_specs = (
        P("lat", "lon", None),
        P("lat", "lon", None),
        P(),
        P(None, "lat", None, None),
        P(),
        P("lat"),
    )
    out_specs = (P("lat", "lon", None), P("lat", None, None))
    return jax.shard_map(
        choose, mesh=mesh, in_specs=in_specs, out_specs=out_specs, check_vma=False
    )
```

```python
import functools

import jax
import jax.numpy as jnp
import numpy as np
from jax import lax
from jax.experimental import pallas as pl
from jax.experimental.pallas import tpu as pltpu
from jax.sharding import PartitionSpec as P

RADIUS = 1
REACH = 2
POLAR = 2


def padded(cells, sides, width, closed):
    for axis, dim in sides:
        count = lax.axis_size(axis)
        ends = count if closed else count - 1
        head = lax.slice_in_dim(cells, 0, width, axis=dim)
        tail = lax.slice_in_dim(cells, cells.shape[dim] - width, cells.shape[dim], axis=dim)
        cells = jnp.concatenate(
            [
                lax.ppermute(tail, axis, [(i, (i + 1) % count) for i in range(ends)]),
                cells,
                lax.ppermute(head, axis, [((i + 1) % count, i) for i in range(ends)]),
            ],
            axis=dim,
        )
    return cells


def from_behind(block, axis, distance):
    devices = range(lax.axis_size(axis))
    route = [((i - distance) % len(devices), i) for i in devices]
    return lax.ppermute(block, axis, route)


def on_device(features, cotangent, weights, basis, polar_kernel, lon_reach):
    lat_rows, lon_cols, channels = features.shape
    kernels = weights.shape[0]
    lat_count = lax.axis_size("lat")
    lon_count = lax.axis_size("lon")
    lat_index = lax.axis_index("lat")
    lon_index = lax.axis_index("lon")
    at_north = lat_index == 0
    at_south = lat_index == lat_count - 1
    at_pole = jnp.logical_or(at_north, at_south)
    lon_total = lon_cols * lon_count
    own_cols = lon_index * lon_cols + jnp.arange(lon_cols, dtype=jnp.int32)
    offsets = jnp.abs(jnp.arange(2 * REACH + 1, dtype=jnp.int32) - REACH)
    reach_mask = (offsets[None, :] <= lon_reach[:, None]).astype(basis.dtype)
    masked = basis * reach_mask[None, :, None, :]
    neighbours = padded(features, (("lat", 0),), RADIUS, False)
    partner_rows = from_behind(
        (features[:RADIUS], features[lat_rows - RADIUS :]), "lon", lon_count // 2
    )
    upper_rows = jnp.where(at_north, partner_rows[0][::-1], neighbours[:RADIUS])
    lower_rows = jnp.where(at_south, partner_rows[1][::-1], neighbours[lat_rows + RADIUS :])
    lengthened = jnp.concatenate([upper_rows, features, lower_rows], 0)
    widened = padded(lengthened, (("lon", 1),), REACH, True)
    basis_sum = jnp.zeros((kernels, lat_rows, lon_cols, channels), jnp.float32)
    for row_off in range(2 * RADIUS + 1):
        windows = jnp.stack(
            [
                widened[row_off : row_off + lat_rows, col_off : col_off + lon_cols]
                for col_off in range(2 * REACH + 1)
            ],
            1,
        )
        basis_sum = basis_sum + jnp.einsum(
            "kib,ibjc->kijc", masked[:, :, row_off], windows, preferred_element_type=jnp.float32
        )
    hemisphere = jnp.where(at_north, polar_kernel[:, 0], polar_kernel[:, 1])
    polar_in = jnp.where(at_north, features[:POLAR], features[lat_rows - POLAR :])
    polar_zero = jnp.zeros((kernels, POLAR, lon_cols, channels), jnp.float32)
    block_rows = lax.all_gather(polar_in, "lon", axis=1, tiled=True)

    def compute():
        source = jnp.arange(block_rows.shape[1], dtype=jnp.int32)
        offset_idx = (source[:, None] - own_cols[None, :]) % lon_total
        circulant = jnp.take(hemisphere, offset_idx, axis=3)
        return jnp.einsum(
            "kabuj,buc->kajc",
            circulant,
            block_rows.astype(jnp.float32),
            precision=lax.Precision.HIGHEST,
        )

    polar_out = lax.cond(at_pole, compute, lambda: polar_zero)
    basis_sum = basis_sum.at[:, :POLAR].add(jnp.where(at_north, polar_out, 0.0))
    basis_sum = basis_sum.at[:, lat_rows - POLAR :].add(jnp.where(at_south, polar_out, 0.0))
    contracted = basis_sum.astype(jnp.bfloat16)
    band_grad = lax.psum_scatter(
        jnp.einsum("kijc,ijo->kco", contracted, cotangent, preferred_element_type=jnp.float32),
        "lat",
        scatter_dimension=0,
        tiled=True,
    )
    grad_weights = lax.psum(band_grad, "lon")
    grad_basis = jnp.einsum(
        "kco,ijo->kijc", weights, cotangent, preferred_element_type=jnp.float32
    ).astype(jnp.bfloat16)
    grad_wide = jnp.zeros((lat_rows + 2 * RADIUS, lon_cols + 2 * REACH, channels), jnp.float32)
    for row_off in range(2 * RADIUS + 1):
        grad_win = jnp.einsum(
            "kib,kijc->ibjc", masked[:, :, row_off], grad_basis, preferred_element_type=jnp.float32
        )
        for col_off in range(2 * REACH + 1):
            grad_wide = grad_wide.at[
                row_off : row_off + lat_rows, col_off : col_off + lon_cols
            ].add(grad_win[:, col_off])
    lon_rims = jnp.concatenate([grad_wide[:, :REACH], grad_wide[:, lon_cols + REACH :]], 1)
    beside_all = padded(lon_rims, (("lon", 1),), REACH, True)
    folded = grad_wide[:, REACH : lon_cols + REACH]
    folded = folded.at[:, :REACH].add(beside_all[:, :REACH])
    folded = folded.at[:, lon_cols - REACH :].add(beside_all[:, 3 * REACH :])
    ghosts = jnp.concatenate([folded[:RADIUS], folded[lat_rows + RADIUS :]], 0)
    beside = padded(ghosts, (("lat", 0),), RADIUS, False)
    turned = from_behind((folded[:RADIUS], folded[lat_rows + RADIUS :]), "lon", lon_count // 2)
    interior = folded[RADIUS : lat_rows + RADIUS]
    from_above = jnp.where(at_north, turned[0][::-1], beside[:RADIUS])
    from_below = jnp.where(at_south, turned[1][::-1], beside[3 * RADIUS :])
    interior = interior.at[:RADIUS].add(from_above)
    interior = interior.at[lat_rows - RADIUS :].add(from_below)
    polar_cot = jnp.where(at_north, cotangent[:POLAR], cotangent[lat_rows - POLAR :])
    running = jnp.zeros((POLAR, lon_cols, channels), jnp.float32)
    add_block_rows = lax.all_gather(polar_cot, "lon", axis=1, tiled=True)

    def compute():
        source = jnp.arange(add_block_rows.shape[1], dtype=jnp.int32)
        offset_idx = (own_cols[None, :] - source[:, None]) % lon_total
        circulant = jnp.take(hemisphere, offset_idx, axis=3)
        block_grad = jnp.einsum(
            "kco,auo->kauc", weights, add_block_rows, preferred_element_type=jnp.float32
        ).astype(jnp.bfloat16)
        return jnp.einsum(
            "kabuj,kauc->bjc",
            circulant,
            block_grad.astype(jnp.float32),
            precision=lax.Precision.HIGHEST,
        )

    polar_grad = lax.cond(at_pole, compute, lambda: running)
    interior = interior.at[:POLAR].add(jnp.where(at_north, polar_grad, 0.0))
    interior = interior.at[lat_rows - POLAR :].add(jnp.where(at_south, polar_grad, 0.0))
    return (interior.astype(jnp.bfloat16), grad_weights)


COLS = 8
SLOTS = 32
MESH = pl.DeviceIdType.MESH


def spread_matrices():
    taps = 2 * REACH + 1
    forward = np.zeros((16, 2, COLS, 4, SLOTS), np.float32)
    backward = np.zeros((16, 2, COLS, 4, SLOTS), np.float32)
    for inner in range(2):
        for col in range(COLS):
            for row in range(4):
                for slot in range(SLOTS):
                    a, b = row - inner, slot - COLS - col + REACH
                    if 0 <= a < 3 and 0 <= b < taps:
                        forward[a * taps + b, inner, col, row, slot] = 1
                    a, b = inner - row + 2, col + REACH - (slot - COLS)
                    if 0 <= a < 3 and 0 <= b < taps:
                        backward[a * taps + b, inner, col, row, slot] = 1
    return np.concatenate([forward.reshape(16, -1), backward.reshape(16, -1)], 1)


def split(values):
    high = values.astype(jnp.bfloat16)
    return high, (values - high.astype(jnp.float32)).astype(jnp.bfloat16)


def mul(a, b, dims=((1,), (0,))):
    return lax.dot_general(a, b, (dims, ((), ())), preferred_element_type=jnp.float32)


def fused(
    n, f_ref, c_ref, w_ref, m_ref, h_ref, d_ref, gf_ref, gw_ref,
    fc, polar, packs, sides, below, rims, near, taps_f, taps_b, rev, circ, ext, sums, own,
    sib_out, sib_in, part, terms, mine, acc,
    send_polar, recv_polar, send_misc, recv_misc, send_sib, recv_sib,
    send_rs, recv_rs, send_ag, recv_ag,
):
    f32, bf16 = jnp.float32, jnp.bfloat16
    lat, lon = lax.axis_index("lat"), lax.axis_index("lon")
    points, channels = f_ref.shape
    rows = points // COLS
    pairs = rows // 2
    kernels = w_ref.shape[0]
    half_k = kernels // 2
    chunk = half_k * channels // n
    window = 4 * SLOTS
    lanes = 16 * window
    other = 1 - lat
    north = lat == 0

    def turn(t):
        return lax.rem(lon + t, n)

    barrier = pltpu.get_barrier_semaphore()
    for t in range(1, n):
        pl.semaphore_signal(barrier, inc=1, device_id=(lat, turn(t)), device_id_type=MESH)
    for t in (0, 1, n - 1):
        pl.semaphore_signal(barrier, inc=1, device_id=(other, turn(t)), device_id_type=MESH)

    fc[0] = f_ref[...]
    fc[1] = c_ref[...]
    place = lax.broadcasted_iota(jnp.int32, (COLS, channels), 0) // REACH
    group = COLS // REACH
    for field in range(2):
        cells = fc[field].astype(f32)
        for side in range(2):
            packed = []
            for g in range(rows // group):
                block = jnp.zeros((COLS, channels), f32)
                for u in range(group):
                    row = cells[COLS * (group * g + u) : COLS * (group * g + u + 1)]
                    shift = REACH * u + (REACH if side == 0 else 0)
                    block = jnp.where(place == u, pltpu.roll(row, shift % COLS, 0), block)
                packed.append(block)
            packs[side, field] = jnp.concatenate(packed, 0).astype(bf16)
    by_row = [m_ref[pl.ds(i, kernels, stride=rows), :] for i in range(rows)]
    rims[...] = jnp.where(north, by_row[-1], by_row[0])
    pl.semaphore_wait(barrier, n + 2)

    def push(src, dst, send, recv, to):
        copy = pltpu.make_async_remote_copy(
            src_ref=src, dst_ref=dst, send_sem=send, recv_sem=recv, device_id=to, device_id_type=MESH
        )
        copy.start()
        return copy

    pole_at = pl.multiple_of(lat * (points - 16), 16)
    edge_at = pl.multiple_of(other * (points - 16), 16)
    arriving = []
    for field in range(2):
        edge = fc.at[field, pl.ds(edge_at, 16)]
        pole = fc.at[field, pl.ds(pole_at, 16)]
        copies = []
        for t in sorted(range(1, n), key=lambda t: -min(t, n - t)):
            copies.append(
                push(
                    pole, polar.at[field, n - t],
                    send_polar.at[field, t], recv_polar.at[field, n - t], (lat, turn(t)),
                )
            )
        routes = (
            (packs.at[0, field], sides.at[0, field], (lat, turn(1))),
            (packs.at[1, field], sides.at[1, field], (lat, turn(n - 1))),
            (edge, below.at[field, 0], (other, turn(1))),
            (edge, below.at[field, 2], (other, turn(n - 1))),
            (edge, below.at[field, 1], (other, lon)),
        )
        for r, (src, dst, to) in enumerate(routes):
            copies.append(push(src, dst, send_misc.at[field, r], recv_misc.at[field, r], to))
        arriving.append(copies)
        polar[field, 0] = fc[field, pl.ds(pole_at, 16)]
    arriving[1].append(push(rims, near, send_misc.at[0, 5], recv_misc.at[0, 5], (other, lon)))

    mat = jnp.concatenate(by_row, 0)
    taps_f[...] = mul(mat[:, :16].astype(bf16), d_ref[:, :lanes]).astype(bf16).astype(f32)
    zonal = [
        [h_ref[pl.ds(lat * 4 + a * 2 + r, kernels, stride=8), :] for r in range(2)] for a in range(2)
    ]
    rolled = [
        jnp.concatenate([pltpu.roll(z, j, 1) if j else z for z in zonal[a]], 1)
        for a in range(2)
        for j in range(COLS)
    ]
    high, low = split(jnp.concatenate(rolled, 0))

    def extend(field):
        gathered = polar[field].astype(f32).reshape(n, 2, COLS, channels)
        pole_rows = [gathered[:, r].reshape(n * COLS, channels) for r in range(2)]
        zeros = jnp.zeros((COLS, channels), f32)
        left, right = sides[0, field].astype(f32), sides[1, field].astype(f32)
        cells = fc[field].astype(f32)
        for i in range(rows):
            g, u = i // group, i % group
            ends = [side[COLS * g : COLS * (g + 1)] for side in (left, right)]
            line = [
                pltpu.roll(ends[0], (COLS - REACH - REACH * u) % COLS, 0),
                cells[COLS * i : COLS * (i + 1)],
                pltpu.roll(ends[1], (COLS - REACH * u) % COLS, 0),
                zeros,
            ]
            ext[field, pl.ds((i + 1) * SLOTS, SLOTS)] = jnp.concatenate(line, 0).astype(bf16)
        turned = gathered[n // 2 - 1 : n // 2 + 2]
        turned = jnp.where(north, turned[:, 0], turned[:, 1])
        beside = below[field].astype(f32).reshape(3, 2, COLS, channels)
        beside = jnp.where(north, beside[:, 0], beside[:, 1])
        top = jnp.where(north, turned, beside).reshape(3 * COLS, channels)
        bottom = jnp.where(north, beside, turned).reshape(3 * COLS, channels)
        ext[field, pl.ds(0, SLOTS)] = jnp.concatenate([top, zeros], 0).astype(bf16)
        ext[field, pl.ds((rows + 1) * SLOTS, SLOTS)] = jnp.concatenate([bottom, zeros], 0).astype(bf16)
        return jnp.concatenate(pole_rows, 0).astype(bf16)

    for copy in arriving[0]:
        copy.wait()
    poles = extend(0)
    polar_part = mul(high, poles) + mul(low, poles)
    for p in range(pairs):
        taps = [
            taps_f[kernels * (2 * p + x // COLS) : kernels * (2 * p + x // COLS + 1),
                   x * window : (x + 1) * window]
            for x in range(16)
        ]
        taps = jnp.concatenate(taps, 0).astype(bf16)
        value = mul(taps, ext[0, pl.ds(2 * p * SLOTS, window)])
        if p == 0:
            value = value + jnp.where(north, polar_part, 0.0)
        if p == pairs - 1:
            value = value + jnp.where(north, 0.0, polar_part)
        for h in range(channels // 128):
            sums[h, pl.ds(16 * kernels * p, 16 * kernels)] = value[:, 128 * h : 128 * (h + 1)]

    cot = c_ref[...]

    def gradient(k):
        cells = [sums[h, pl.ds(k, points, stride=kernels), :] for h in range(channels // 128)]
        return mul(jnp.concatenate(cells, 1).astype(bf16), cot, ((0,), (0,)))

    to_sib = []
    for j in range(half_k):
        at = pl.ds(j * channels, channels)
        sib_out[at] = gradient(other * half_k + j).astype(bf16)
        to_sib.append(
            push(sib_out.at[at], sib_in.at[at], send_sib.at[j], recv_sib.at[j], (other, lon))
        )
    for j in range(half_k):
        own[pl.ds(j * channels, channels)] = gradient(lat * half_k + j)
    for j in range(half_k):
        at = pl.ds(j * channels, channels)
        to_sib[j].wait()
        part[at] = (own[at] + sib_in[at].astype(f32)).astype(bf16)
    scatter = []
    for t in range(1, n):
        at = pl.ds(pl.multiple_of(turn(t) * chunk, chunk), chunk)
        scatter.append(
            push(part.at[at], terms.at[t], send_rs.at[t], recv_rs.at[t], (lat, turn(t)))
        )

    for copy in arriving[1]:
        copy.wait()
    poles = extend(1)
    taps_each = 3 * (2 * REACH + 1)
    step = 2 * (2 * REACH + 1)
    lane = lax.broadcasted_iota(jnp.int32, (kernels, 128), 1)
    first_taps = lane < taps_each - step
    up = jnp.where(first_taps, by_row[0], 0.0)
    up = pltpu.roll(up, step, 1)
    down = pltpu.roll(by_row[-1], 128 - step, 1)
    down = jnp.where(first_taps, down, 0.0)
    beside = near[...]
    mat = jnp.concatenate(
        [jnp.where(north, up, beside)] + by_row + [jnp.where(north, beside, down)], 0
    )
    spread = mul(mat[:, :16].astype(bf16), d_ref[:, lanes:])
    part_of = lax.broadcasted_iota(jnp.int32, (kernels, window), 1) // SLOTS
    for p in range(pairs):
        for x in range(16):
            tile = jnp.zeros((kernels, window), f32)
            for q in range(4):
                i = kernels * (2 * p + q)
                tile = jnp.where(
                    part_of == q, spread[i : i + kernels, x * window : (x + 1) * window], tile
                )
            taps_b[pl.ds((16 * p + x) * kernels, kernels)] = tile
    flip = lax.broadcasted_iota(jnp.int32, (128, 128), 0) + lax.broadcasted_iota(
        jnp.int32, (128, 128), 1
    )
    flip = jnp.where(flip == 127, 1.0, 0.0).astype(bf16)
    high, low = split(h_ref[...])
    rev[...] = mul(high, flip) + mul(low, flip)
    for r in range(2):
        turned = [
            rev[pl.ds(lat * 4 + a * 2 + r, kernels, stride=8), :] for a in range(2)
        ]
        for j in range(COLS):
            for a in range(2):
                circ[a, pl.ds((r * COLS + j) * kernels, kernels)] = pltpu.roll(turned[a], j + 1, 1)
    acc[...] = jnp.zeros_like(acc)

    def per_kernel(k, pole_acc):
        weight = w_ref[k]
        grad = mul(ext[1], weight, ((1,), (1,))).astype(bf16)
        for p in range(pairs):
            taps = taps_b[pl.ds(16 * kernels * p + k, 16, stride=kernels), :].astype(bf16)
            acc[pl.ds(16 * p, 16)] += mul(taps, grad[2 * p * SLOTS : 2 * p * SLOTS + window])
        pole_grad = mul(poles, weight, ((1,), (1,))).astype(bf16)
        high, low = split(
            jnp.concatenate([circ[a, pl.ds(k, 16, stride=kernels), :] for a in range(2)], 1)
        )
        return pole_acc + mul(high, pole_grad) + mul(low, pole_grad)

    pole_acc = lax.fori_loop(0, kernels, per_kernel, jnp.zeros((16, channels), f32))
    acc[pl.ds(0, 16)] += jnp.where(north, pole_acc, 0.0)
    acc[pl.ds(points - 16, 16)] += jnp.where(north, 0.0, pole_acc)
    gf_ref[...] = acc[...].astype(bf16)

    here = pl.ds(pl.multiple_of(lon * chunk, chunk), chunk)
    total = part[here].astype(f32)
    for t in range(1, n):
        scatter[t - 1].wait()
        total = total + terms[t].astype(f32)
    mine[...] = total.astype(bf16)
    gw_ref[here] = mine[...]
    gather = []
    for t in range(1, n):
        gather.append(push(mine, gw_ref.at[here], send_ag.at[t], recv_ag.at[t], (lat, turn(t))))
    for copy in gather:
        copy.wait()


def in_kernel(features, cotangent, weights, basis, polar_kernel, lon_reach):
    lat_rows, lon_cols, channels = features.shape
    kernels = weights.shape[0]
    n = lax.axis_size("lon")
    pairs, points = lat_rows // 2, lat_rows * lon_cols
    taps = 3 * (2 * REACH + 1)
    bf16, f32 = jnp.bfloat16, jnp.float32
    offsets = jnp.abs(jnp.arange(2 * REACH + 1, dtype=jnp.int32) - REACH)
    reach_mask = offsets[None, :] <= lon_reach[:, None]
    masked = jnp.where(reach_mask[None, :, None, :], basis, 0)
    masked = masked.reshape(kernels * lat_rows, taps).astype(f32)
    masked = jnp.pad(masked, ((0, 0), (0, 128 - taps)))
    spread = jnp.asarray(spread_matrices(), bf16)
    half = kernels * channels // 2
    window, pack = 4 * SLOTS, lat_rows * REACH
    dma = pltpu.SemaphoreType.DMA
    vmem = pl.BlockSpec(memory_space=pltpu.VMEM)
    grad_features, grad_weights = pl.pallas_call(
        functools.partial(fused, n),
        out_shape=(
            jax.ShapeDtypeStruct((points, channels), bf16),
            jax.ShapeDtypeStruct((half, channels), bf16),
        ),
        in_specs=[vmem] * 6,
        out_specs=(vmem, vmem),
        scratch_shapes=[
            pltpu.VMEM((2, points, channels), bf16),
            pltpu.VMEM((2, n, 16, channels), bf16),
            pltpu.VMEM((2, 2, pack, channels), bf16),
            pltpu.VMEM((2, 2, pack, channels), bf16),
            pltpu.VMEM((2, 3, 16, channels), bf16),
            pltpu.VMEM((kernels, 128), f32),
            pltpu.VMEM((kernels, 128), f32),
            pltpu.VMEM((lat_rows * kernels, 16 * window), f32),
            pltpu.VMEM((pairs * 16 * kernels, window), f32),
            pltpu.VMEM((kernels * 8, 128), f32),
            pltpu.VMEM((2, 16 * kernels, lon_cols * n), f32),
            pltpu.VMEM((2, (lat_rows + 2) * SLOTS, channels), bf16),
            pltpu.VMEM((channels // 128, points * kernels, 128), f32),
            pltpu.VMEM((half, channels), f32),
            pltpu.VMEM((half, channels), bf16),
            pltpu.VMEM((half, channels), bf16),
            pltpu.VMEM((half, channels), bf16),
            pltpu.VMEM((n, half // n, channels), bf16),
            pltpu.VMEM((half // n, channels), bf16),
            pltpu.VMEM((points, channels), f32),
            dma((2, n)), dma((2, n)), dma((2, 6)), dma((2, 6)), dma((4,)), dma((4,)),
            dma((n,)), dma((n,)), dma((n,)), dma((n,)),
        ],
        compiler_params=pltpu.CompilerParams(
            collective_id=0, has_side_effects=True, vmem_limit_bytes=40 * 2**20
        ),
    )(
        features.reshape(points, channels), cotangent.reshape(points, channels),
        weights, masked, polar_kernel.reshape(kernels * 8, lon_cols * n), spread,
    )
    return (
        grad_features.reshape(features.shape),
        grad_weights.astype(f32).reshape(kernels // 2, channels, channels),
    )


def choose(features, cotangent, weights, basis, polar_kernel, lon_reach):
    rows, cols, channels = features.shape
    n = lax.axis_size("lon")
    kernels = weights.shape[0]
    fits = (
        lax.axis_size("lat") == 2 and cols == COLS and n * COLS == 128 and rows % 8 == 0
        and kernels == 8 and (kernels // 2 * channels) % (16 * n) == 0
    )
    plan = in_kernel if fits else on_device
    return plan(features, cotangent, weights, basis, polar_kernel, lon_reach)


def solution(mesh):
    in_specs = (
        P("lat", "lon", None),
        P("lat", "lon", None),
        P(),
        P(None, "lat", None, None),
        P(),
        P("lat"),
    )
    out_specs = (P("lat", "lon", None), P("lat", None, None))
    return jax.shard_map(
        choose, mesh=mesh, in_specs=in_specs, out_specs=out_specs, check_vma=False
    )
```

```python
import functools

import jax
import jax.numpy as jnp
import numpy as np
from jax import lax
from jax.experimental import pallas as pl
from jax.experimental.pallas import tpu as pltpu
from jax.sharding import PartitionSpec as P

RADIUS = 1
REACH = 2
POLAR = 2


def padded(cells, sides, width, closed):
    for axis, dim in sides:
        count = lax.axis_size(axis)
        ends = count if closed else count - 1
        head = lax.slice_in_dim(cells, 0, width, axis=dim)
        tail = lax.slice_in_dim(cells, cells.shape[dim] - width, cells.shape[dim], axis=dim)
        cells = jnp.concatenate(
            [
                lax.ppermute(tail, axis, [(i, (i + 1) % count) for i in range(ends)]),
                cells,
                lax.ppermute(head, axis, [((i + 1) % count, i) for i in range(ends)]),
            ],
            axis=dim,
        )
    return cells


def from_behind(block, axis, distance):
    devices = range(lax.axis_size(axis))
    route = [((i - distance) % len(devices), i) for i in devices]
    return lax.ppermute(block, axis, route)


def on_device(features, cotangent, weights, basis, polar_kernel, lon_reach):
    lat_rows, lon_cols, channels = features.shape
    kernels = weights.shape[0]
    lat_count = lax.axis_size("lat")
    lon_count = lax.axis_size("lon")
    lat_index = lax.axis_index("lat")
    lon_index = lax.axis_index("lon")
    at_north = lat_index == 0
    at_south = lat_index == lat_count - 1
    at_pole = jnp.logical_or(at_north, at_south)
    lon_total = lon_cols * lon_count
    own_cols = lon_index * lon_cols + jnp.arange(lon_cols, dtype=jnp.int32)
    offsets = jnp.abs(jnp.arange(2 * REACH + 1, dtype=jnp.int32) - REACH)
    reach_mask = (offsets[None, :] <= lon_reach[:, None]).astype(basis.dtype)
    masked = basis * reach_mask[None, :, None, :]
    neighbours = padded(features, (("lat", 0),), RADIUS, False)
    partner_rows = from_behind(
        (features[:RADIUS], features[lat_rows - RADIUS :]), "lon", lon_count // 2
    )
    upper_rows = jnp.where(at_north, partner_rows[0][::-1], neighbours[:RADIUS])
    lower_rows = jnp.where(at_south, partner_rows[1][::-1], neighbours[lat_rows + RADIUS :])
    lengthened = jnp.concatenate([upper_rows, features, lower_rows], 0)
    widened = padded(lengthened, (("lon", 1),), REACH, True)
    basis_sum = jnp.zeros((kernels, lat_rows, lon_cols, channels), jnp.float32)
    for row_off in range(2 * RADIUS + 1):
        windows = jnp.stack(
            [
                widened[row_off : row_off + lat_rows, col_off : col_off + lon_cols]
                for col_off in range(2 * REACH + 1)
            ],
            1,
        )
        basis_sum = basis_sum + jnp.einsum(
            "kib,ibjc->kijc", masked[:, :, row_off], windows, preferred_element_type=jnp.float32
        )
    hemisphere = jnp.where(at_north, polar_kernel[:, 0], polar_kernel[:, 1])
    polar_in = jnp.where(at_north, features[:POLAR], features[lat_rows - POLAR :])
    polar_zero = jnp.zeros((kernels, POLAR, lon_cols, channels), jnp.float32)
    block_rows = lax.all_gather(polar_in, "lon", axis=1, tiled=True)

    def compute():
        source = jnp.arange(block_rows.shape[1], dtype=jnp.int32)
        offset_idx = (source[:, None] - own_cols[None, :]) % lon_total
        circulant = jnp.take(hemisphere, offset_idx, axis=3)
        return jnp.einsum(
            "kabuj,buc->kajc",
            circulant,
            block_rows.astype(jnp.float32),
            precision=lax.Precision.HIGHEST,
        )

    polar_out = lax.cond(at_pole, compute, lambda: polar_zero)
    basis_sum = basis_sum.at[:, :POLAR].add(jnp.where(at_north, polar_out, 0.0))
    basis_sum = basis_sum.at[:, lat_rows - POLAR :].add(jnp.where(at_south, polar_out, 0.0))
    contracted = basis_sum.astype(jnp.bfloat16)
    band_grad = lax.psum_scatter(
        jnp.einsum("kijc,ijo->kco", contracted, cotangent, preferred_element_type=jnp.float32),
        "lat",
        scatter_dimension=0,
        tiled=True,
    )
    grad_weights = lax.psum(band_grad, "lon")
    grad_basis = jnp.einsum(
        "kco,ijo->kijc", weights, cotangent, preferred_element_type=jnp.float32
    ).astype(jnp.bfloat16)
    grad_wide = jnp.zeros((lat_rows + 2 * RADIUS, lon_cols + 2 * REACH, channels), jnp.float32)
    for row_off in range(2 * RADIUS + 1):
        grad_win = jnp.einsum(
            "kib,kijc->ibjc", masked[:, :, row_off], grad_basis, preferred_element_type=jnp.float32
        )
        for col_off in range(2 * REACH + 1):
            grad_wide = grad_wide.at[
                row_off : row_off + lat_rows, col_off : col_off + lon_cols
            ].add(grad_win[:, col_off])
    lon_rims = jnp.concatenate([grad_wide[:, :REACH], grad_wide[:, lon_cols + REACH :]], 1)
    beside_all = padded(lon_rims, (("lon", 1),), REACH, True)
    folded = grad_wide[:, REACH : lon_cols + REACH]
    folded = folded.at[:, :REACH].add(beside_all[:, :REACH])
    folded = folded.at[:, lon_cols - REACH :].add(beside_all[:, 3 * REACH :])
    ghosts = jnp.concatenate([folded[:RADIUS], folded[lat_rows + RADIUS :]], 0)
    beside = padded(ghosts, (("lat", 0),), RADIUS, False)
    turned = from_behind((folded[:RADIUS], folded[lat_rows + RADIUS :]), "lon", lon_count // 2)
    interior = folded[RADIUS : lat_rows + RADIUS]
    from_above = jnp.where(at_north, turned[0][::-1], beside[:RADIUS])
    from_below = jnp.where(at_south, turned[1][::-1], beside[3 * RADIUS :])
    interior = interior.at[:RADIUS].add(from_above)
    interior = interior.at[lat_rows - RADIUS :].add(from_below)
    polar_cot = jnp.where(at_north, cotangent[:POLAR], cotangent[lat_rows - POLAR :])
    running = jnp.zeros((POLAR, lon_cols, channels), jnp.float32)
    add_block_rows = lax.all_gather(polar_cot, "lon", axis=1, tiled=True)

    def compute():
        source = jnp.arange(add_block_rows.shape[1], dtype=jnp.int32)
        offset_idx = (own_cols[None, :] - source[:, None]) % lon_total
        circulant = jnp.take(hemisphere, offset_idx, axis=3)
        block_grad = jnp.einsum(
            "kco,auo->kauc", weights, add_block_rows, preferred_element_type=jnp.float32
        ).astype(jnp.bfloat16)
        return jnp.einsum(
            "kabuj,kauc->bjc",
            circulant,
            block_grad.astype(jnp.float32),
            precision=lax.Precision.HIGHEST,
        )

    polar_grad = lax.cond(at_pole, compute, lambda: running)
    interior = interior.at[:POLAR].add(jnp.where(at_north, polar_grad, 0.0))
    interior = interior.at[lat_rows - POLAR :].add(jnp.where(at_south, polar_grad, 0.0))
    return (interior.astype(jnp.bfloat16), grad_weights)


GROUP = 4
COLS = 8
SLOTS = 32
MESH = pl.DeviceIdType.MESH


def spread_matrices():
    taps = 2 * REACH + 1
    forward = np.zeros((16, 2, COLS, 4, SLOTS), np.float32)
    backward = np.zeros((16, 2, COLS, 4, SLOTS), np.float32)
    for inner in range(2):
        for col in range(COLS):
            for row in range(4):
                for slot in range(SLOTS):
                    a, b = row - inner, slot - COLS - col + REACH
                    if 0 <= a < 3 and 0 <= b < taps:
                        forward[a * taps + b, inner, col, row, slot] = 1
                    a, b = inner - row + 2, col + REACH - (slot - COLS)
                    if 0 <= a < 3 and 0 <= b < taps:
                        backward[a * taps + b, inner, col, row, slot] = 1
    return np.concatenate([forward.reshape(16, -1), backward.reshape(16, -1)], 1)


def split(values):
    high = values.astype(jnp.bfloat16)
    return high, (values - high.astype(jnp.float32)).astype(jnp.bfloat16)


def mul(a, b, dims=((1,), (0,))):
    return lax.dot_general(a, b, (dims, ((), ())), preferred_element_type=jnp.float32)


def fused(
    n, f_ref, c_ref, w_hbm, m_ref, reach_ref, h_ref, d_hbm, gf_ref, gw_ref,
    w_ref, d_ref, load_sem, basis_in,
    fc, polar, packs, sides, below, rims, near, taps_f, taps_b, rev, circ, ext, sums, own,
    sib_out, sib_in, part, plane_terms, plane_sums, line_terms, mine, acc,
    send_polar, recv_polar, send_misc, recv_misc, send_sib, recv_sib,
    send_plane, recv_plane, send_line, recv_line,
    send_copy, recv_copy, send_first, recv_first,
):
    f32, bf16 = jnp.float32, jnp.bfloat16
    lat, lon = lax.axis_index("lat"), lax.axis_index("lon")
    points, channels = f_ref.shape
    rows = points // COLS
    pairs = rows // 2
    kernels = w_ref.shape[0]
    lines = n // GROUP
    half_k = kernels // 2
    chunk = half_k * channels // n
    window = 4 * SLOTS
    lanes = 16 * window
    other = 1 - lat
    north = lat == 0

    def turn(t):
        return lax.rem(lon + t, n)

    loads = [
        pltpu.make_async_copy(src, dst, load_sem.at[i])
        for i, (src, dst) in enumerate(((d_hbm, d_ref), (w_hbm, w_ref)))
    ]
    for load in loads:
        load.start()
    barrier = pltpu.get_barrier_semaphore()
    for t in range(1, n):
        pl.semaphore_signal(barrier, inc=1, device_id=(lat, turn(t)), device_id_type=MESH)
    for t in (0, 1, n - 1):
        pl.semaphore_signal(barrier, inc=1, device_id=(other, turn(t)), device_id_type=MESH)

    fc[0] = f_ref[...]
    fc[1] = c_ref[...]
    place = lax.broadcasted_iota(jnp.int32, (COLS, channels), 0) // REACH
    group = COLS // REACH
    for field in range(2):
        cells = fc[field].astype(f32)
        for side in range(2):
            packed = []
            for g in range(rows // group):
                block = jnp.zeros((COLS, channels), f32)
                for u in range(group):
                    row = cells[COLS * (group * g + u) : COLS * (group * g + u + 1)]
                    shift = REACH * u + (REACH if side == 0 else 0)
                    block = jnp.where(place == u, pltpu.roll(row, shift % COLS, 0), block)
                packed.append(block)
            packs[side, field] = jnp.concatenate(packed, 0).astype(bf16)
    span = 2 * REACH + 1
    basis_in[...] = jnp.zeros_like(basis_in)
    basis_in[:, : 3 * span] = m_ref[...].astype(f32)
    lane = lax.broadcasted_iota(jnp.int32, (kernels, 128), 1)
    away = jnp.abs(lax.rem(lane, span) - REACH)
    by_row = [
        jnp.where(away <= reach_ref[i], basis_in[pl.ds(i, kernels, stride=rows), :], 0.0)
        for i in range(rows)
    ]
    rims[...] = jnp.where(north, by_row[-1], by_row[0])
    pl.semaphore_wait(barrier, n + 2)

    def push(src, dst, send, recv, to):
        copy = pltpu.make_async_remote_copy(
            src_ref=src, dst_ref=dst, send_sem=send, recv_sem=recv, device_id=to, device_id_type=MESH
        )
        copy.start()
        return copy

    pole_at = pl.multiple_of(lat * (points - 16), 16)
    edge_at = pl.multiple_of(other * (points - 16), 16)

    def send_field(field):
        edge = fc.at[field, pl.ds(edge_at, 16)]
        pole = fc.at[field, pl.ds(pole_at, 16)]
        copies = []
        for t in sorted(range(1, n), key=lambda t: -min(t, n - t)):
            copies.append(
                push(
                    pole, polar.at[field, n - t],
                    send_polar.at[field, t], recv_polar.at[field, n - t], (lat, turn(t)),
                )
            )
        routes = (
            (packs.at[0, field], sides.at[0, field], (lat, turn(1))),
            (packs.at[1, field], sides.at[1, field], (lat, turn(n - 1))),
            (edge, below.at[field, 0], (other, turn(1))),
            (edge, below.at[field, 2], (other, turn(n - 1))),
            (edge, below.at[field, 1], (other, lon)),
        )
        for r, (src, dst, to) in enumerate(routes):
            copies.append(push(src, dst, send_misc.at[field, r], recv_misc.at[field, r], to))
        polar[field, 0] = fc[field, pl.ds(pole_at, 16)]
        return copies

    field_copies = send_field(0)
    loads[0].wait()
    mat = jnp.concatenate(by_row, 0)
    taps_f[...] = mul(mat[:, :16].astype(bf16), d_ref[:, :lanes]).astype(bf16).astype(f32)
    zonal = [
        [h_ref[pl.ds(lat * 4 + a * 2 + r, kernels, stride=8), :] for r in range(2)] for a in range(2)
    ]
    rolled = [
        jnp.concatenate([pltpu.roll(z, j, 1) if j else z for z in zonal[a]], 1)
        for a in range(2)
        for j in range(COLS)
    ]
    high, low = split(jnp.concatenate(rolled, 0))

    def extend(field):
        gathered = polar[field].astype(f32).reshape(n, 2, COLS, channels)
        pole_rows = [gathered[:, r].reshape(n * COLS, channels) for r in range(2)]
        zeros = jnp.zeros((COLS, channels), f32)
        left, right = sides[0, field].astype(f32), sides[1, field].astype(f32)
        cells = fc[field].astype(f32)
        for i in range(rows):
            g, u = i // group, i % group
            ends = [side[COLS * g : COLS * (g + 1)] for side in (left, right)]
            line = [
                pltpu.roll(ends[0], (COLS - REACH - REACH * u) % COLS, 0),
                cells[COLS * i : COLS * (i + 1)],
                pltpu.roll(ends[1], (COLS - REACH * u) % COLS, 0),
                zeros,
            ]
            ext[field, pl.ds((i + 1) * SLOTS, SLOTS)] = jnp.concatenate(line, 0).astype(bf16)
        turned = gathered[n // 2 - 1 : n // 2 + 2]
        turned = jnp.where(north, turned[:, 0], turned[:, 1])
        beside = below[field].astype(f32).reshape(3, 2, COLS, channels)
        beside = jnp.where(north, beside[:, 0], beside[:, 1])
        top = jnp.where(north, turned, beside).reshape(3 * COLS, channels)
        bottom = jnp.where(north, beside, turned).reshape(3 * COLS, channels)
        ext[field, pl.ds(0, SLOTS)] = jnp.concatenate([top, zeros], 0).astype(bf16)
        ext[field, pl.ds((rows + 1) * SLOTS, SLOTS)] = jnp.concatenate([bottom, zeros], 0).astype(bf16)
        return jnp.concatenate(pole_rows, 0).astype(bf16)

    for copy in field_copies:
        copy.wait()
    cotangent_copies = send_field(1)
    cotangent_copies.append(push(rims, near, send_misc.at[0, 5], recv_misc.at[0, 5], (other, lon)))
    poles = extend(0)
    polar_part = mul(high, poles) + mul(low, poles)
    for p in range(pairs):
        taps = [
            taps_f[kernels * (2 * p + x // COLS) : kernels * (2 * p + x // COLS + 1),
                   x * window : (x + 1) * window]
            for x in range(16)
        ]
        taps = jnp.concatenate(taps, 0).astype(bf16)
        value = mul(taps, ext[0, pl.ds(2 * p * SLOTS, window)])
        if p == 0:
            value = value + jnp.where(north, polar_part, 0.0)
        if p == pairs - 1:
            value = value + jnp.where(north, 0.0, polar_part)
        for h in range(channels // 128):
            sums[h, pl.ds(16 * kernels * p, 16 * kernels)] = value[:, 128 * h : 128 * (h + 1)]

    cot = c_ref[...]

    def gradient(k):
        cells = [sums[h, pl.ds(k, points, stride=kernels), :] for h in range(channels // 128)]
        return mul(jnp.concatenate(cells, 1).astype(bf16), cot, ((0,), (0,)))

    line, spot = lon // GROUP, lax.rem(lon, GROUP)

    def in_plane(t):
        return (lat, line * GROUP + lax.rem(spot + t, GROUP))

    def on_line(t):
        return (lat, lax.rem(line + t, lines) * GROUP + spot)

    def rows_of(line_at, spot_at):
        return pl.ds(pl.multiple_of((line_at * GROUP + spot_at) * chunk, chunk), chunk)

    order = list(range(1, lines)) + [0]
    to_sib = {}
    for t in order:
        j = lax.rem(line + t, lines)
        sib_out[t] = gradient(other * half_k + j).astype(bf16)
        to_sib[t] = push(sib_out.at[t], sib_in.at[t], send_sib.at[t], recv_sib.at[t], (other, lon))
    for t in order:
        own[t] = gradient(lat * half_k + lax.rem(line + t, lines))
    plane = {}
    for t in order:
        j = lax.rem(line + t, lines)
        to_sib[t].wait()
        part[pl.ds(pl.multiple_of(j * channels, channels), channels)] = (
            own[t] + sib_in[t].astype(f32)
        ).astype(bf16)
        plane[t] = [
            push(
                part.at[rows_of(j, lax.rem(spot + u, GROUP))], plane_terms.at[u, t],
                send_plane.at[u, t], recv_plane.at[u, t], in_plane(u),
            )
            for u in range(1, GROUP)
        ]
    taps_each = 3 * (2 * REACH + 1)
    step = 2 * (2 * REACH + 1)
    first_taps = lane < taps_each - step
    up = jnp.where(first_taps, by_row[0], 0.0)
    up = pltpu.roll(up, step, 1)
    down = pltpu.roll(by_row[-1], 128 - step, 1)
    down = jnp.where(first_taps, down, 0.0)
    cotangent_copies[-1].wait()
    beside = near[...]
    mat = jnp.concatenate(
        [jnp.where(north, up, beside)] + by_row + [jnp.where(north, beside, down)], 0
    )
    spread = mul(mat[:, :16].astype(bf16), d_ref[:, lanes:])
    part_of = lax.broadcasted_iota(jnp.int32, (kernels, window), 1) // SLOTS
    for p in range(pairs):
        for x in range(16):
            tile = jnp.zeros((kernels, window), f32)
            for q in range(4):
                i = kernels * (2 * p + q)
                tile = jnp.where(
                    part_of == q, spread[i : i + kernels, x * window : (x + 1) * window], tile
                )
            taps_b[pl.ds((16 * p + x) * kernels, kernels)] = tile
    flip = lax.broadcasted_iota(jnp.int32, (128, 128), 0) + lax.broadcasted_iota(
        jnp.int32, (128, 128), 1
    )
    flip = jnp.where(flip == 127, 1.0, 0.0).astype(bf16)
    high, low = split(h_ref[...])
    rev[...] = mul(high, flip) + mul(low, flip)
    for r in range(2):
        turned = [
            rev[pl.ds(lat * 4 + a * 2 + r, kernels, stride=8), :] for a in range(2)
        ]
        for j in range(COLS):
            for a in range(2):
                circ[a, pl.ds((r * COLS + j) * kernels, kernels)] = pltpu.roll(turned[a], j + 1, 1)
    along = {}
    for t in order:
        total = part[rows_of(lax.rem(line + t, lines), spot)].astype(f32)
        for u in range(1, GROUP):
            plane[t][u - 1].wait()
            total = total + plane_terms[u, t].astype(f32)
        if t:
            plane_sums[t] = total.astype(bf16)
            along[t] = push(
                plane_sums.at[t], line_terms.at[t], send_line.at[t], recv_line.at[t], on_line(t)
            )

    acc[...] = jnp.zeros_like(acc)
    for copy in cotangent_copies[:-1]:
        copy.wait()
    poles = extend(1)
    loads[1].wait()

    def per_kernel(k, pole_acc):
        weight = w_ref[k]
        grad = mul(ext[1], weight, ((1,), (1,))).astype(bf16)
        for p in range(pairs):
            taps = taps_b[pl.ds(16 * kernels * p + k, 16, stride=kernels), :].astype(bf16)
            acc[pl.ds(16 * p, 16)] += mul(taps, grad[2 * p * SLOTS : 2 * p * SLOTS + window])
        pole_grad = mul(poles, weight, ((1,), (1,))).astype(bf16)
        high, low = split(
            jnp.concatenate([circ[a, pl.ds(k, 16, stride=kernels), :] for a in range(2)], 1)
        )
        return pole_acc + mul(high, pole_grad) + mul(low, pole_grad)

    pole_acc = lax.fori_loop(0, kernels, per_kernel, jnp.zeros((16, channels), f32))
    acc[pl.ds(0, 16)] += jnp.where(north, pole_acc, 0.0)
    acc[pl.ds(points - 16, 16)] += jnp.where(north, 0.0, pole_acc)
    gf_ref[...] = acc[...].astype(bf16)

    here = rows_of(line, spot)
    for t in range(1, lines):
        along[t].wait()
        total = total + line_terms[t].astype(f32)
    mine[...] = total.astype(bf16)
    gw_ref[here] = mine[...]

    def spread_plane(src, at, t):
        return [
            push(src, gw_ref.at[at], send_copy.at[u, t], recv_copy.at[u, t], in_plane(u))
            for u in range(1, GROUP)
        ]

    first = [
        push(mine, gw_ref.at[here], send_first.at[t], recv_first.at[t], on_line(t))
        for t in range(1, lines)
    ]
    gather = spread_plane(mine, here, 0)
    for t in range(1, lines):
        first[t - 1].wait()
        at = rows_of(lax.rem(line - t + lines, lines), spot)
        gather += spread_plane(gw_ref.at[at], at, t)
    for copy in gather:
        copy.wait()


def in_kernel(features, cotangent, weights, basis, polar_kernel, lon_reach):
    lat_rows, lon_cols, channels = features.shape
    kernels = weights.shape[0]
    n = lax.axis_size("lon")
    pairs, points = lat_rows // 2, lat_rows * lon_cols
    taps = 3 * (2 * REACH + 1)
    bf16, f32 = jnp.bfloat16, jnp.float32
    masked = basis.reshape(kernels * lat_rows, taps)
    spread = jnp.asarray(spread_matrices(), bf16)
    half = kernels * channels // 2
    window, pack = 4 * SLOTS, lat_rows * REACH
    dma = pltpu.SemaphoreType.DMA
    vmem = pl.BlockSpec(memory_space=pltpu.VMEM)
    hbm = pl.BlockSpec(memory_space=pl.ANY)
    lines = n // GROUP
    grad_features, grad_weights = pl.pallas_call(
        functools.partial(fused, n),
        out_shape=(
            jax.ShapeDtypeStruct((points, channels), bf16),
            jax.ShapeDtypeStruct((half, channels), bf16),
        ),
        in_specs=[vmem, vmem, hbm, vmem, pl.BlockSpec(memory_space=pltpu.SMEM), vmem, hbm],
        out_specs=(vmem, vmem),
        scratch_shapes=[
            pltpu.VMEM(weights.shape, bf16),
            pltpu.VMEM(spread.shape, bf16),
            dma((2,)),
            pltpu.VMEM((kernels * lat_rows, 128), f32),
            pltpu.VMEM((2, points, channels), bf16),
            pltpu.VMEM((2, n, 16, channels), bf16),
            pltpu.VMEM((2, 2, pack, channels), bf16),
            pltpu.VMEM((2, 2, pack, channels), bf16),
            pltpu.VMEM((2, 3, 16, channels), bf16),
            pltpu.VMEM((kernels, 128), f32),
            pltpu.VMEM((kernels, 128), f32),
            pltpu.VMEM((lat_rows * kernels, 16 * window), f32),
            pltpu.VMEM((pairs * 16 * kernels, window), f32),
            pltpu.VMEM((kernels * 8, 128), f32),
            pltpu.VMEM((2, 16 * kernels, lon_cols * n), f32),
            pltpu.VMEM((2, (lat_rows + 2) * SLOTS, channels), bf16),
            pltpu.VMEM((channels // 128, points * kernels, 128), f32),
            pltpu.VMEM((lines, channels, channels), f32),
            pltpu.VMEM((lines, channels, channels), bf16),
            pltpu.VMEM((lines, channels, channels), bf16),
            pltpu.VMEM((half, channels), bf16),
            pltpu.VMEM((GROUP, lines, half // n, channels), bf16),
            pltpu.VMEM((lines, half // n, channels), bf16),
            pltpu.VMEM((lines, half // n, channels), bf16),
            pltpu.VMEM((half // n, channels), bf16),
            pltpu.VMEM((points, channels), f32),
            dma((2, n)), dma((2, n)), dma((2, 6)), dma((2, 6)), dma((4,)), dma((4,)),
            dma((GROUP, lines)), dma((GROUP, lines)), dma((lines,)), dma((lines,)),
            dma((GROUP, lines)), dma((GROUP, lines)), dma((lines,)), dma((lines,)),
        ],
        compiler_params=pltpu.CompilerParams(
            collective_id=0, has_side_effects=True, vmem_limit_bytes=56 * 2**20
        ),
    )(
        features.reshape(points, channels), cotangent.reshape(points, channels),
        weights, masked, lon_reach, polar_kernel.reshape(kernels * 8, lon_cols * n), spread,
    )
    return (
        grad_features.reshape(features.shape),
        grad_weights.astype(f32).reshape(kernels // 2, channels, channels),
    )


def choose(features, cotangent, weights, basis, polar_kernel, lon_reach):
    rows, cols, channels = features.shape
    n = lax.axis_size("lon")
    kernels = weights.shape[0]
    fits = (
        lax.axis_size("lat") == 2 and cols == COLS and n * COLS == 128 and n == GROUP * (kernels // 2) and rows % 8 == 0
        and kernels == 8 and (kernels // 2 * channels) % (16 * n) == 0
    )
    plan = in_kernel if fits else on_device
    return plan(features, cotangent, weights, basis, polar_kernel, lon_reach)


def solution(mesh):
    in_specs = (
        P("lat", "lon", None),
        P("lat", "lon", None),
        P(),
        P(None, "lat", None, None),
        P(),
        P("lat"),
    )
    out_specs = (P("lat", "lon", None), P("lat", None, None))
    return jax.shard_map(
        choose, mesh=mesh, in_specs=in_specs, out_specs=out_specs, check_vma=False
    )
```

```python
import functools

import jax
import jax.numpy as jnp
import numpy as np
from jax import lax
from jax.experimental import pallas as pl
from jax.experimental.pallas import tpu as pltpu
from jax.sharding import PartitionSpec as P

RADIUS = 1
REACH = 2
POLAR = 2


def padded(cells, sides, width, closed):
    for axis, dim in sides:
        count = lax.axis_size(axis)
        ends = count if closed else count - 1
        head = lax.slice_in_dim(cells, 0, width, axis=dim)
        tail = lax.slice_in_dim(cells, cells.shape[dim] - width, cells.shape[dim], axis=dim)
        cells = jnp.concatenate(
            [
                lax.ppermute(tail, axis, [(i, (i + 1) % count) for i in range(ends)]),
                cells,
                lax.ppermute(head, axis, [((i + 1) % count, i) for i in range(ends)]),
            ],
            axis=dim,
        )
    return cells


def from_behind(block, axis, distance):
    devices = range(lax.axis_size(axis))
    route = [((i - distance) % len(devices), i) for i in devices]
    return lax.ppermute(block, axis, route)


def on_device(features, cotangent, weights, basis, polar_kernel, lon_reach):
    lat_rows, lon_cols, channels = features.shape
    kernels = weights.shape[0]
    lat_count = lax.axis_size("lat")
    lon_count = lax.axis_size("lon")
    lat_index = lax.axis_index("lat")
    lon_index = lax.axis_index("lon")
    at_north = lat_index == 0
    at_south = lat_index == lat_count - 1
    at_pole = jnp.logical_or(at_north, at_south)
    lon_total = lon_cols * lon_count
    own_cols = lon_index * lon_cols + jnp.arange(lon_cols, dtype=jnp.int32)
    offsets = jnp.abs(jnp.arange(2 * REACH + 1, dtype=jnp.int32) - REACH)
    reach_mask = (offsets[None, :] <= lon_reach[:, None]).astype(basis.dtype)
    masked = basis * reach_mask[None, :, None, :]
    neighbours = padded(features, (("lat", 0),), RADIUS, False)
    partner_rows = from_behind(
        (features[:RADIUS], features[lat_rows - RADIUS :]), "lon", lon_count // 2
    )
    upper_rows = jnp.where(at_north, partner_rows[0][::-1], neighbours[:RADIUS])
    lower_rows = jnp.where(at_south, partner_rows[1][::-1], neighbours[lat_rows + RADIUS :])
    lengthened = jnp.concatenate([upper_rows, features, lower_rows], 0)
    widened = padded(lengthened, (("lon", 1),), REACH, True)
    basis_sum = jnp.zeros((kernels, lat_rows, lon_cols, channels), jnp.float32)
    for row_off in range(2 * RADIUS + 1):
        windows = jnp.stack(
            [
                widened[row_off : row_off + lat_rows, col_off : col_off + lon_cols]
                for col_off in range(2 * REACH + 1)
            ],
            1,
        )
        basis_sum = basis_sum + jnp.einsum(
            "kib,ibjc->kijc", masked[:, :, row_off], windows, preferred_element_type=jnp.float32
        )
    hemisphere = jnp.where(at_north, polar_kernel[:, 0], polar_kernel[:, 1])
    polar_in = jnp.where(at_north, features[:POLAR], features[lat_rows - POLAR :])
    polar_zero = jnp.zeros((kernels, POLAR, lon_cols, channels), jnp.float32)
    block_rows = lax.all_gather(polar_in, "lon", axis=1, tiled=True)

    def compute():
        source = jnp.arange(block_rows.shape[1], dtype=jnp.int32)
        offset_idx = (source[:, None] - own_cols[None, :]) % lon_total
        circulant = jnp.take(hemisphere, offset_idx, axis=3)
        return jnp.einsum(
            "kabuj,buc->kajc",
            circulant,
            block_rows.astype(jnp.float32),
            precision=lax.Precision.HIGHEST,
        )

    polar_out = lax.cond(at_pole, compute, lambda: polar_zero)
    basis_sum = basis_sum.at[:, :POLAR].add(jnp.where(at_north, polar_out, 0.0))
    basis_sum = basis_sum.at[:, lat_rows - POLAR :].add(jnp.where(at_south, polar_out, 0.0))
    contracted = basis_sum.astype(jnp.bfloat16)
    band_grad = lax.psum_scatter(
        jnp.einsum("kijc,ijo->kco", contracted, cotangent, preferred_element_type=jnp.float32),
        "lat",
        scatter_dimension=0,
        tiled=True,
    )
    grad_weights = lax.psum(band_grad, "lon")
    grad_basis = jnp.einsum(
        "kco,ijo->kijc", weights, cotangent, preferred_element_type=jnp.float32
    ).astype(jnp.bfloat16)
    grad_wide = jnp.zeros((lat_rows + 2 * RADIUS, lon_cols + 2 * REACH, channels), jnp.float32)
    for row_off in range(2 * RADIUS + 1):
        grad_win = jnp.einsum(
            "kib,kijc->ibjc", masked[:, :, row_off], grad_basis, preferred_element_type=jnp.float32
        )
        for col_off in range(2 * REACH + 1):
            grad_wide = grad_wide.at[
                row_off : row_off + lat_rows, col_off : col_off + lon_cols
            ].add(grad_win[:, col_off])
    lon_rims = jnp.concatenate([grad_wide[:, :REACH], grad_wide[:, lon_cols + REACH :]], 1)
    beside_all = padded(lon_rims, (("lon", 1),), REACH, True)
    folded = grad_wide[:, REACH : lon_cols + REACH]
    folded = folded.at[:, :REACH].add(beside_all[:, :REACH])
    folded = folded.at[:, lon_cols - REACH :].add(beside_all[:, 3 * REACH :])
    ghosts = jnp.concatenate([folded[:RADIUS], folded[lat_rows + RADIUS :]], 0)
    beside = padded(ghosts, (("lat", 0),), RADIUS, False)
    turned = from_behind((folded[:RADIUS], folded[lat_rows + RADIUS :]), "lon", lon_count // 2)
    interior = folded[RADIUS : lat_rows + RADIUS]
    from_above = jnp.where(at_north, turned[0][::-1], beside[:RADIUS])
    from_below = jnp.where(at_south, turned[1][::-1], beside[3 * RADIUS :])
    interior = interior.at[:RADIUS].add(from_above)
    interior = interior.at[lat_rows - RADIUS :].add(from_below)
    polar_cot = jnp.where(at_north, cotangent[:POLAR], cotangent[lat_rows - POLAR :])
    running = jnp.zeros((POLAR, lon_cols, channels), jnp.float32)
    add_block_rows = lax.all_gather(polar_cot, "lon", axis=1, tiled=True)

    def compute():
        source = jnp.arange(add_block_rows.shape[1], dtype=jnp.int32)
        offset_idx = (own_cols[None, :] - source[:, None]) % lon_total
        circulant = jnp.take(hemisphere, offset_idx, axis=3)
        block_grad = jnp.einsum(
            "kco,auo->kauc", weights, add_block_rows, preferred_element_type=jnp.float32
        ).astype(jnp.bfloat16)
        return jnp.einsum(
            "kabuj,kauc->bjc",
            circulant,
            block_grad.astype(jnp.float32),
            precision=lax.Precision.HIGHEST,
        )

    polar_grad = lax.cond(at_pole, compute, lambda: running)
    interior = interior.at[:POLAR].add(jnp.where(at_north, polar_grad, 0.0))
    interior = interior.at[lat_rows - POLAR :].add(jnp.where(at_south, polar_grad, 0.0))
    return (interior.astype(jnp.bfloat16), grad_weights)


GROUP = 4
COLS = 8
SLOTS = 32
MESH = pl.DeviceIdType.MESH


def spread_matrices():
    taps = 2 * REACH + 1
    forward = np.zeros((16, 2, COLS, 4, SLOTS), np.float32)
    backward = np.zeros((16, 2, COLS, 4, SLOTS), np.float32)
    for inner in range(2):
        for col in range(COLS):
            for row in range(4):
                for slot in range(SLOTS):
                    a, b = row - inner, slot - COLS - col + REACH
                    if 0 <= a < 3 and 0 <= b < taps:
                        forward[a * taps + b, inner, col, row, slot] = 1
                    a, b = inner - row + 2, col + REACH - (slot - COLS)
                    if 0 <= a < 3 and 0 <= b < taps:
                        backward[a * taps + b, inner, col, row, slot] = 1
    return np.concatenate([forward.reshape(16, -1), backward.reshape(16, -1)], 1)


def split(values):
    high = values.astype(jnp.bfloat16)
    return high, (values - high.astype(jnp.float32)).astype(jnp.bfloat16)


def mul(a, b, dims=((1,), (0,))):
    return lax.dot_general(a, b, (dims, ((), ())), preferred_element_type=jnp.float32)


def fused(
    n, f_hbm, c_hbm, w_hbm, m_hbm, reach_ref, h_hbm, d_hbm, gf_ref, gw_ref,
    w_ref, m_ref, h_ref, d_ref, load_sem, basis_in,
    fc, polar, packs, sides, below, rims, near, taps_f, taps_b, rev, circ, ext, sums, own,
    sib_out, sib_in, part, plane_terms, plane_sums, line_terms, mine, acc,
    send_polar, recv_polar, send_misc, recv_misc, send_sib, recv_sib,
    send_plane, recv_plane, send_line, recv_line,
    send_copy, recv_copy, send_first, recv_first,
):
    f32, bf16 = jnp.float32, jnp.bfloat16
    lat, lon = lax.axis_index("lat"), lax.axis_index("lon")
    points, channels = f_hbm.shape
    rows = points // COLS
    pairs = rows // 2
    kernels = w_ref.shape[0]
    lines = n // GROUP
    half_k = kernels // 2
    chunk = half_k * channels // n
    window = 4 * SLOTS
    lanes = 16 * window
    other = 1 - lat
    north = lat == 0

    def turn(t):
        return lax.rem(lon + t, n)

    barrier = pltpu.get_barrier_semaphore()
    for t in range(1, n):
        pl.semaphore_signal(barrier, inc=1, device_id=(lat, turn(t)), device_id_type=MESH)
    for t in (0, 1, n - 1):
        pl.semaphore_signal(barrier, inc=1, device_id=(other, turn(t)), device_id_type=MESH)

    sources = (f_hbm, c_hbm, m_hbm, d_hbm, h_hbm, w_hbm)
    places = (fc.at[0], fc.at[1], m_ref, d_ref, h_ref, w_ref)
    loads = [
        pltpu.make_async_copy(src, dst, load_sem.at[i])
        for i, (src, dst) in enumerate(zip(sources, places))
    ]
    for load in loads:
        load.start()
    for load in loads[:3]:
        load.wait()
    place = lax.broadcasted_iota(jnp.int32, (COLS, channels), 0) // REACH
    group = COLS // REACH
    for field in range(2):
        cells = fc[field].astype(f32)
        for side in range(2):
            packed = []
            for g in range(rows // group):
                block = jnp.zeros((COLS, channels), f32)
                for u in range(group):
                    row = cells[COLS * (group * g + u) : COLS * (group * g + u + 1)]
                    shift = REACH * u + (REACH if side == 0 else 0)
                    block = jnp.where(place == u, pltpu.roll(row, shift % COLS, 0), block)
                packed.append(block)
            packs[side, field] = jnp.concatenate(packed, 0).astype(bf16)
    span = 2 * REACH + 1
    basis_in[...] = jnp.zeros_like(basis_in)
    basis_in[:, : 3 * span] = m_ref[...].astype(f32)
    lane = lax.broadcasted_iota(jnp.int32, (kernels, 128), 1)
    away = jnp.abs(lax.rem(lane, span) - REACH)
    by_row = [
        jnp.where(away <= reach_ref[i], basis_in[pl.ds(i, kernels, stride=rows), :], 0.0)
        for i in range(rows)
    ]
    rims[...] = jnp.where(north, by_row[-1], by_row[0])
    pl.semaphore_wait(barrier, n + 2)

    def push(src, dst, send, recv, to):
        copy = pltpu.make_async_remote_copy(
            src_ref=src, dst_ref=dst, send_sem=send, recv_sem=recv, device_id=to, device_id_type=MESH
        )
        copy.start()
        return copy

    pole_at = pl.multiple_of(lat * (points - 16), 16)
    edge_at = pl.multiple_of(other * (points - 16), 16)

    def send_field(field):
        edge = fc.at[field, pl.ds(edge_at, 16)]
        pole = fc.at[field, pl.ds(pole_at, 16)]
        copies = []
        for t in sorted(range(1, n), key=lambda t: -min(t, n - t)):
            copies.append(
                push(
                    pole, polar.at[field, n - t],
                    send_polar.at[field, t], recv_polar.at[field, n - t], (lat, turn(t)),
                )
            )
        routes = (
            (packs.at[0, field], sides.at[0, field], (lat, turn(1))),
            (packs.at[1, field], sides.at[1, field], (lat, turn(n - 1))),
            (edge, below.at[field, 0], (other, turn(1))),
            (edge, below.at[field, 2], (other, turn(n - 1))),
            (edge, below.at[field, 1], (other, lon)),
        )
        for r, (src, dst, to) in enumerate(routes):
            copies.append(push(src, dst, send_misc.at[field, r], recv_misc.at[field, r], to))
        polar[field, 0] = fc[field, pl.ds(pole_at, 16)]
        return copies

    field_copies = send_field(0)
    loads[3].wait()
    loads[4].wait()
    mat = jnp.concatenate(by_row, 0)
    taps_f[...] = mul(mat[:, :16].astype(bf16), d_ref[:, :lanes]).astype(bf16).astype(f32)
    zonal = [
        [h_ref[pl.ds(lat * 4 + a * 2 + r, kernels, stride=8), :] for r in range(2)] for a in range(2)
    ]
    rolled = [
        jnp.concatenate([pltpu.roll(z, j, 1) if j else z for z in zonal[a]], 1)
        for a in range(2)
        for j in range(COLS)
    ]
    high, low = split(jnp.concatenate(rolled, 0))

    def extend(field):
        gathered = polar[field].astype(f32).reshape(n, 2, COLS, channels)
        pole_rows = [gathered[:, r].reshape(n * COLS, channels) for r in range(2)]
        zeros = jnp.zeros((COLS, channels), f32)
        left, right = sides[0, field].astype(f32), sides[1, field].astype(f32)
        cells = fc[field].astype(f32)
        for i in range(rows):
            g, u = i // group, i % group
            ends = [side[COLS * g : COLS * (g + 1)] for side in (left, right)]
            line = [
                pltpu.roll(ends[0], (COLS - REACH - REACH * u) % COLS, 0),
                cells[COLS * i : COLS * (i + 1)],
                pltpu.roll(ends[1], (COLS - REACH * u) % COLS, 0),
                zeros,
            ]
            ext[field, pl.ds((i + 1) * SLOTS, SLOTS)] = jnp.concatenate(line, 0).astype(bf16)
        turned = gathered[n // 2 - 1 : n // 2 + 2]
        turned = jnp.where(north, turned[:, 0], turned[:, 1])
        beside = below[field].astype(f32).reshape(3, 2, COLS, channels)
        beside = jnp.where(north, beside[:, 0], beside[:, 1])
        top = jnp.where(north, turned, beside).reshape(3 * COLS, channels)
        bottom = jnp.where(north, beside, turned).reshape(3 * COLS, channels)
        ext[field, pl.ds(0, SLOTS)] = jnp.concatenate([top, zeros], 0).astype(bf16)
        ext[field, pl.ds((rows + 1) * SLOTS, SLOTS)] = jnp.concatenate([bottom, zeros], 0).astype(bf16)
        return jnp.concatenate(pole_rows, 0).astype(bf16)

    flip = lax.broadcasted_iota(jnp.int32, (128, 128), 0) + lax.broadcasted_iota(
        jnp.int32, (128, 128), 1
    )
    flip = jnp.where(flip == 127, 1.0, 0.0).astype(bf16)
    flip_high, flip_low = split(h_ref[...])
    rev[...] = mul(flip_high, flip) + mul(flip_low, flip)
    for r in range(2):
        turned = [
            rev[pl.ds(lat * 4 + a * 2 + r, kernels, stride=8), :] for a in range(2)
        ]
        for j in range(COLS):
            for a in range(2):
                circ[a, pl.ds((r * COLS + j) * kernels, kernels)] = pltpu.roll(turned[a], j + 1, 1)
    for copy in field_copies:
        copy.wait()
    cotangent_copies = send_field(1)
    cotangent_copies.append(push(rims, near, send_misc.at[0, 5], recv_misc.at[0, 5], (other, lon)))
    poles = extend(0)
    polar_part = mul(high, poles) + mul(low, poles)
    for p in range(pairs):
        taps = [
            taps_f[kernels * (2 * p + x // COLS) : kernels * (2 * p + x // COLS + 1),
                   x * window : (x + 1) * window]
            for x in range(16)
        ]
        taps = jnp.concatenate(taps, 0).astype(bf16)
        value = mul(taps, ext[0, pl.ds(2 * p * SLOTS, window)])
        if p == 0:
            value = value + jnp.where(north, polar_part, 0.0)
        if p == pairs - 1:
            value = value + jnp.where(north, 0.0, polar_part)
        for h in range(channels // 128):
            sums[h, pl.ds(16 * kernels * p, 16 * kernels)] = value[:, 128 * h : 128 * (h + 1)]

    cot = fc[1]

    def gradient(k):
        cells = [sums[h, pl.ds(k, points, stride=kernels), :] for h in range(channels // 128)]
        return mul(jnp.concatenate(cells, 1).astype(bf16), cot, ((0,), (0,)))

    line, spot = lon // GROUP, lax.rem(lon, GROUP)

    def in_plane(t):
        return (lat, line * GROUP + lax.rem(spot + t, GROUP))

    def on_line(t):
        return (lat, lax.rem(line + t, lines) * GROUP + spot)

    def rows_of(line_at, spot_at):
        return pl.ds(pl.multiple_of((line_at * GROUP + spot_at) * chunk, chunk), chunk)

    order = list(range(1, lines)) + [0]
    to_sib = {}
    for t in order:
        j = lax.rem(line + t, lines)
        sib_out[t] = gradient(other * half_k + j).astype(bf16)
        to_sib[t] = push(sib_out.at[t], sib_in.at[t], send_sib.at[t], recv_sib.at[t], (other, lon))
    for t in order:
        own[t] = gradient(lat * half_k + lax.rem(line + t, lines))
    plane = {}
    for t in order:
        j = lax.rem(line + t, lines)
        to_sib[t].wait()
        part[pl.ds(pl.multiple_of(j * channels, channels), channels)] = (
            own[t] + sib_in[t].astype(f32)
        ).astype(bf16)
        plane[t] = [
            push(
                part.at[rows_of(j, lax.rem(spot + u, GROUP))], plane_terms.at[u, t],
                send_plane.at[u, t], recv_plane.at[u, t], in_plane(u),
            )
            for u in range(1, GROUP)
        ]
    taps_each = 3 * (2 * REACH + 1)
    step = 2 * (2 * REACH + 1)
    first_taps = lane < taps_each - step
    up = jnp.where(first_taps, by_row[0], 0.0)
    up = pltpu.roll(up, step, 1)
    down = pltpu.roll(by_row[-1], 128 - step, 1)
    down = jnp.where(first_taps, down, 0.0)
    cotangent_copies[-1].wait()
    beside = near[...]
    mat = jnp.concatenate(
        [jnp.where(north, up, beside)] + by_row + [jnp.where(north, beside, down)], 0
    )
    spread = mul(mat[:, :16].astype(bf16), d_ref[:, lanes:])
    part_of = lax.broadcasted_iota(jnp.int32, (kernels, window), 1) // SLOTS
    for p in range(pairs):
        for x in range(16):
            tile = jnp.zeros((kernels, window), f32)
            for q in range(4):
                i = kernels * (2 * p + q)
                tile = jnp.where(
                    part_of == q, spread[i : i + kernels, x * window : (x + 1) * window], tile
                )
            taps_b[pl.ds((16 * p + x) * kernels, kernels)] = tile
    along = {}
    for t in order:
        total = part[rows_of(lax.rem(line + t, lines), spot)].astype(f32)
        for u in range(1, GROUP):
            plane[t][u - 1].wait()
            total = total + plane_terms[u, t].astype(f32)
        if t:
            plane_sums[t] = total.astype(bf16)
            along[t] = push(
                plane_sums.at[t], line_terms.at[t], send_line.at[t], recv_line.at[t], on_line(t)
            )

    acc[...] = jnp.zeros_like(acc)
    for copy in cotangent_copies[:-1]:
        copy.wait()
    poles = extend(1)
    loads[5].wait()

    def per_kernel(k, pole_acc):
        weight = w_ref[k]
        grad = mul(ext[1], weight, ((1,), (1,))).astype(bf16)
        for p in range(pairs):
            taps = taps_b[pl.ds(16 * kernels * p + k, 16, stride=kernels), :].astype(bf16)
            acc[pl.ds(16 * p, 16)] += mul(taps, grad[2 * p * SLOTS : 2 * p * SLOTS + window])
        pole_grad = mul(poles, weight, ((1,), (1,))).astype(bf16)
        high, low = split(
            jnp.concatenate([circ[a, pl.ds(k, 16, stride=kernels), :] for a in range(2)], 1)
        )
        return pole_acc + mul(high, pole_grad) + mul(low, pole_grad)

    pole_acc = jnp.zeros((16, channels), f32)
    pole_acc = lax.fori_loop(0, 3, per_kernel, pole_acc)
    here = rows_of(line, spot)
    for t in range(1, lines):
        along[t].wait()
        total = total + line_terms[t].astype(f32)
    mine[...] = total.astype(bf16)
    gw_ref[here] = mine[...]

    def spread_plane(src, at, t):
        return [
            push(src, gw_ref.at[at], send_copy.at[u, t], recv_copy.at[u, t], in_plane(u))
            for u in range(1, GROUP)
        ]

    near_first = sorted(range(1, lines), key=lambda t: min(t, lines - t))
    first = {
        t: push(mine, gw_ref.at[here], send_first.at[t], recv_first.at[t], on_line(t))
        for t in near_first
    }
    gather = spread_plane(mine, here, 0)
    done = 3
    for t in near_first:
        pole_acc = per_kernel(done, pole_acc)
        done += 1
        first[t].wait()
        at = rows_of(lax.rem(line - t + lines, lines), spot)
        gather += spread_plane(gw_ref.at[at], at, t)
    pole_acc = lax.fori_loop(done, kernels, per_kernel, pole_acc)
    acc[pl.ds(0, 16)] += jnp.where(north, pole_acc, 0.0)
    acc[pl.ds(points - 16, 16)] += jnp.where(north, 0.0, pole_acc)
    gf_ref[...] = acc[...].astype(bf16)
    for copy in gather:
        copy.wait()


def in_kernel(features, cotangent, weights, basis, polar_kernel, lon_reach):
    lat_rows, lon_cols, channels = features.shape
    kernels = weights.shape[0]
    n = lax.axis_size("lon")
    pairs, points = lat_rows // 2, lat_rows * lon_cols
    taps = 3 * (2 * REACH + 1)
    bf16, f32 = jnp.bfloat16, jnp.float32
    masked = basis.reshape(kernels * lat_rows, taps)
    spread = jnp.asarray(spread_matrices(), bf16)
    half = kernels * channels // 2
    window, pack = 4 * SLOTS, lat_rows * REACH
    dma = pltpu.SemaphoreType.DMA
    vmem = pl.BlockSpec(memory_space=pltpu.VMEM)
    hbm = pl.BlockSpec(memory_space=pltpu.HBM)
    lines = n // GROUP
    grad_features, grad_weights = pl.pallas_call(
        functools.partial(fused, n),
        out_shape=(
            jax.ShapeDtypeStruct((points, channels), bf16),
            jax.ShapeDtypeStruct((half, channels), bf16),
        ),
        in_specs=[hbm] * 4 + [pl.BlockSpec(memory_space=pltpu.SMEM)] + [hbm] * 2,
        out_specs=(vmem, vmem),
        scratch_shapes=[
            pltpu.VMEM(weights.shape, bf16),
            pltpu.VMEM(masked.shape, bf16),
            pltpu.VMEM((kernels * 8, lon_cols * n), f32),
            pltpu.VMEM(spread.shape, bf16),
            dma((6,)),
            pltpu.VMEM((kernels * lat_rows, 128), f32),
            pltpu.VMEM((2, points, channels), bf16),
            pltpu.VMEM((2, n, 16, channels), bf16),
            pltpu.VMEM((2, 2, pack, channels), bf16),
            pltpu.VMEM((2, 2, pack, channels), bf16),
            pltpu.VMEM((2, 3, 16, channels), bf16),
            pltpu.VMEM((kernels, 128), f32),
            pltpu.VMEM((kernels, 128), f32),
            pltpu.VMEM((lat_rows * kernels, 16 * window), f32),
            pltpu.VMEM((pairs * 16 * kernels, window), f32),
            pltpu.VMEM((kernels * 8, 128), f32),
            pltpu.VMEM((2, 16 * kernels, lon_cols * n), f32),
            pltpu.VMEM((2, (lat_rows + 2) * SLOTS, channels), bf16),
            pltpu.VMEM((channels // 128, points * kernels, 128), f32),
            pltpu.VMEM((lines, channels, channels), f32),
            pltpu.VMEM((lines, channels, channels), bf16),
            pltpu.VMEM((lines, channels, channels), bf16),
            pltpu.VMEM((half, channels), bf16),
            pltpu.VMEM((GROUP, lines, half // n, channels), bf16),
            pltpu.VMEM((lines, half // n, channels), bf16),
            pltpu.VMEM((lines, half // n, channels), bf16),
            pltpu.VMEM((half // n, channels), bf16),
            pltpu.VMEM((points, channels), f32),
            dma((2, n)), dma((2, n)), dma((2, 6)), dma((2, 6)), dma((4,)), dma((4,)),
            dma((GROUP, lines)), dma((GROUP, lines)), dma((lines,)), dma((lines,)),
            dma((GROUP, lines)), dma((GROUP, lines)), dma((lines,)), dma((lines,)),
        ],
        compiler_params=pltpu.CompilerParams(
            collective_id=0, has_side_effects=True, vmem_limit_bytes=56 * 2**20
        ),
    )(
        features.reshape(points, channels), cotangent.reshape(points, channels),
        weights, masked, lon_reach, polar_kernel.reshape(kernels * 8, lon_cols * n), spread,
    )
    return (
        grad_features.reshape(features.shape),
        grad_weights.astype(f32).reshape(kernels // 2, channels, channels),
    )


def choose(features, cotangent, weights, basis, polar_kernel, lon_reach):
    rows, cols, channels = features.shape
    n = lax.axis_size("lon")
    kernels = weights.shape[0]
    fits = (
        lax.axis_size("lat") == 2 and cols == COLS and n * COLS == 128 and n == GROUP * (kernels // 2) and rows % 8 == 0
        and kernels == 8 and (kernels // 2 * channels) % (16 * n) == 0
    )
    plan = in_kernel if fits else on_device
    return plan(features, cotangent, weights, basis, polar_kernel, lon_reach)


def solution(mesh):
    in_specs = (
        P("lat", "lon", None),
        P("lat", "lon", None),
        P(),
        P(None, "lat", None, None),
        P(),
        P("lat"),
    )
    out_specs = (P("lat", "lon", None), P("lat", None, None))
    return jax.shard_map(
        choose, mesh=mesh, in_specs=in_specs, out_specs=out_specs, check_vma=False
    )
```

```python
import functools

import jax
import jax.numpy as jnp
import numpy as np
from jax import lax
from jax.experimental import pallas as pl
from jax.experimental.pallas import tpu as pltpu
from jax.sharding import PartitionSpec as P

RADIUS = 1
REACH = 2
POLAR = 2


def padded(cells, sides, width, closed):
    for axis, dim in sides:
        count = lax.axis_size(axis)
        ends = count if closed else count - 1
        head = lax.slice_in_dim(cells, 0, width, axis=dim)
        tail = lax.slice_in_dim(cells, cells.shape[dim] - width, cells.shape[dim], axis=dim)
        cells = jnp.concatenate(
            [
                lax.ppermute(tail, axis, [(i, (i + 1) % count) for i in range(ends)]),
                cells,
                lax.ppermute(head, axis, [((i + 1) % count, i) for i in range(ends)]),
            ],
            axis=dim,
        )
    return cells


def from_behind(block, axis, distance):
    devices = range(lax.axis_size(axis))
    route = [((i - distance) % len(devices), i) for i in devices]
    return lax.ppermute(block, axis, route)


def on_device(features, cotangent, weights, basis, polar_kernel, lon_reach):
    lat_rows, lon_cols, channels = features.shape
    kernels = weights.shape[0]
    lat_count = lax.axis_size("lat")
    lon_count = lax.axis_size("lon")
    lat_index = lax.axis_index("lat")
    lon_index = lax.axis_index("lon")
    at_north = lat_index == 0
    at_south = lat_index == lat_count - 1
    at_pole = jnp.logical_or(at_north, at_south)
    lon_total = lon_cols * lon_count
    own_cols = lon_index * lon_cols + jnp.arange(lon_cols, dtype=jnp.int32)
    offsets = jnp.abs(jnp.arange(2 * REACH + 1, dtype=jnp.int32) - REACH)
    reach_mask = (offsets[None, :] <= lon_reach[:, None]).astype(basis.dtype)
    masked = basis * reach_mask[None, :, None, :]
    neighbours = padded(features, (("lat", 0),), RADIUS, False)
    partner_rows = from_behind(
        (features[:RADIUS], features[lat_rows - RADIUS :]), "lon", lon_count // 2
    )
    upper_rows = jnp.where(at_north, partner_rows[0][::-1], neighbours[:RADIUS])
    lower_rows = jnp.where(at_south, partner_rows[1][::-1], neighbours[lat_rows + RADIUS :])
    lengthened = jnp.concatenate([upper_rows, features, lower_rows], 0)
    widened = padded(lengthened, (("lon", 1),), REACH, True)
    basis_sum = jnp.zeros((kernels, lat_rows, lon_cols, channels), jnp.float32)
    for row_off in range(2 * RADIUS + 1):
        windows = jnp.stack(
            [
                widened[row_off : row_off + lat_rows, col_off : col_off + lon_cols]
                for col_off in range(2 * REACH + 1)
            ],
            1,
        )
        basis_sum = basis_sum + jnp.einsum(
            "kib,ibjc->kijc", masked[:, :, row_off], windows, preferred_element_type=jnp.float32
        )
    hemisphere = jnp.where(at_north, polar_kernel[:, 0], polar_kernel[:, 1])
    polar_in = jnp.where(at_north, features[:POLAR], features[lat_rows - POLAR :])
    polar_zero = jnp.zeros((kernels, POLAR, lon_cols, channels), jnp.float32)
    block_rows = lax.all_gather(polar_in, "lon", axis=1, tiled=True)

    def compute():
        source = jnp.arange(block_rows.shape[1], dtype=jnp.int32)
        offset_idx = (source[:, None] - own_cols[None, :]) % lon_total
        circulant = jnp.take(hemisphere, offset_idx, axis=3)
        return jnp.einsum(
            "kabuj,buc->kajc",
            circulant,
            block_rows.astype(jnp.float32),
            precision=lax.Precision.HIGHEST,
        )

    polar_out = lax.cond(at_pole, compute, lambda: polar_zero)
    basis_sum = basis_sum.at[:, :POLAR].add(jnp.where(at_north, polar_out, 0.0))
    basis_sum = basis_sum.at[:, lat_rows - POLAR :].add(jnp.where(at_south, polar_out, 0.0))
    contracted = basis_sum.astype(jnp.bfloat16)
    band_grad = lax.psum_scatter(
        jnp.einsum("kijc,ijo->kco", contracted, cotangent, preferred_element_type=jnp.float32),
        "lat",
        scatter_dimension=0,
        tiled=True,
    )
    grad_weights = lax.psum(band_grad, "lon")
    grad_basis = jnp.einsum(
        "kco,ijo->kijc", weights, cotangent, preferred_element_type=jnp.float32
    ).astype(jnp.bfloat16)
    grad_wide = jnp.zeros((lat_rows + 2 * RADIUS, lon_cols + 2 * REACH, channels), jnp.float32)
    for row_off in range(2 * RADIUS + 1):
        grad_win = jnp.einsum(
            "kib,kijc->ibjc", masked[:, :, row_off], grad_basis, preferred_element_type=jnp.float32
        )
        for col_off in range(2 * REACH + 1):
            grad_wide = grad_wide.at[
                row_off : row_off + lat_rows, col_off : col_off + lon_cols
            ].add(grad_win[:, col_off])
    lon_rims = jnp.concatenate([grad_wide[:, :REACH], grad_wide[:, lon_cols + REACH :]], 1)
    beside_all = padded(lon_rims, (("lon", 1),), REACH, True)
    folded = grad_wide[:, REACH : lon_cols + REACH]
    folded = folded.at[:, :REACH].add(beside_all[:, :REACH])
    folded = folded.at[:, lon_cols - REACH :].add(beside_all[:, 3 * REACH :])
    ghosts = jnp.concatenate([folded[:RADIUS], folded[lat_rows + RADIUS :]], 0)
    beside = padded(ghosts, (("lat", 0),), RADIUS, False)
    turned = from_behind((folded[:RADIUS], folded[lat_rows + RADIUS :]), "lon", lon_count // 2)
    interior = folded[RADIUS : lat_rows + RADIUS]
    from_above = jnp.where(at_north, turned[0][::-1], beside[:RADIUS])
    from_below = jnp.where(at_south, turned[1][::-1], beside[3 * RADIUS :])
    interior = interior.at[:RADIUS].add(from_above)
    interior = interior.at[lat_rows - RADIUS :].add(from_below)
    polar_cot = jnp.where(at_north, cotangent[:POLAR], cotangent[lat_rows - POLAR :])
    running = jnp.zeros((POLAR, lon_cols, channels), jnp.float32)
    add_block_rows = lax.all_gather(polar_cot, "lon", axis=1, tiled=True)

    def compute():
        source = jnp.arange(add_block_rows.shape[1], dtype=jnp.int32)
        offset_idx = (own_cols[None, :] - source[:, None]) % lon_total
        circulant = jnp.take(hemisphere, offset_idx, axis=3)
        block_grad = jnp.einsum(
            "kco,auo->kauc", weights, add_block_rows, preferred_element_type=jnp.float32
        ).astype(jnp.bfloat16)
        return jnp.einsum(
            "kabuj,kauc->bjc",
            circulant,
            block_grad.astype(jnp.float32),
            precision=lax.Precision.HIGHEST,
        )

    polar_grad = lax.cond(at_pole, compute, lambda: running)
    interior = interior.at[:POLAR].add(jnp.where(at_north, polar_grad, 0.0))
    interior = interior.at[lat_rows - POLAR :].add(jnp.where(at_south, polar_grad, 0.0))
    return (interior.astype(jnp.bfloat16), grad_weights)


GROUP = 4
COLS = 8
SLOTS = 32
MESH = pl.DeviceIdType.MESH


def spread_matrices():
    taps = 2 * REACH + 1
    forward = np.zeros((16, 2, COLS, 4, SLOTS), np.float32)
    backward = np.zeros((16, 2, COLS, 4, SLOTS), np.float32)
    for inner in range(2):
        for col in range(COLS):
            for row in range(4):
                for slot in range(SLOTS):
                    a, b = row - inner, slot - COLS - col + REACH
                    if 0 <= a < 3 and 0 <= b < taps:
                        forward[a * taps + b, inner, col, row, slot] = 1
                    a, b = inner - row + 2, col + REACH - (slot - COLS)
                    if 0 <= a < 3 and 0 <= b < taps:
                        backward[a * taps + b, inner, col, row, slot] = 1
    return np.concatenate([forward.reshape(16, -1), backward.reshape(16, -1)], 1)


def split(values):
    high = values.astype(jnp.bfloat16)
    return high, (values - high.astype(jnp.float32)).astype(jnp.bfloat16)


def mul(a, b, dims=((1,), (0,))):
    return lax.dot_general(a, b, (dims, ((), ())), preferred_element_type=jnp.float32)


def fused(
    n, f_hbm, c_hbm, w_hbm, m_hbm, reach_ref, h_hbm, d_hbm, gf_ref, gw_ref,
    w_ref, m_ref, h_ref, d_ref, load_sem, basis_in, basis_by_row,
    fc, polar, packs, sides, below, rims, near, taps_f, taps_b, rev, circ, ext, sums, own,
    sib_out, sib_in, part, plane_terms, plane_sums, line_terms, mine, acc,
    send_polar, recv_polar, send_misc, recv_misc, send_sib, recv_sib,
    send_plane, recv_plane, send_line, recv_line,
    send_copy, recv_copy, send_first, recv_first,
):
    f32, bf16 = jnp.float32, jnp.bfloat16
    lat, lon = lax.axis_index("lat"), lax.axis_index("lon")
    points, channels = f_hbm.shape
    rows = points // COLS
    pairs = rows // 2
    kernels = w_ref.shape[0]
    lines = n // GROUP
    half_k = kernels // 2
    chunk = half_k * channels // n
    window = 4 * SLOTS
    lanes = 16 * window
    other = 1 - lat
    north = lat == 0

    def turn(t):
        return lax.rem(lon + t, n)

    barrier = pltpu.get_barrier_semaphore()
    for t in range(1, n):
        pl.semaphore_signal(barrier, inc=1, device_id=(lat, turn(t)), device_id_type=MESH)
    for t in (0, 1, n - 1):
        pl.semaphore_signal(barrier, inc=1, device_id=(other, turn(t)), device_id_type=MESH)

    sources = (f_hbm, c_hbm, m_hbm, d_hbm, h_hbm, w_hbm)
    places = (fc.at[0], fc.at[1], m_ref, d_ref, h_ref, w_ref)
    loads = [
        pltpu.make_async_copy(src, dst, load_sem.at[i])
        for i, (src, dst) in enumerate(zip(sources, places))
    ]
    for load in loads:
        load.start()
    for load in loads[:3]:
        load.wait()
    place = lax.broadcasted_iota(jnp.int32, (COLS, channels), 0) // REACH
    group = COLS // REACH
    for field in range(2):
        cells = fc[field].astype(f32)
        for side in range(2):
            packed = []
            for g in range(rows // group):
                block = jnp.zeros((COLS, channels), f32)
                for u in range(group):
                    row = cells[COLS * (group * g + u) : COLS * (group * g + u + 1)]
                    shift = REACH * u + (REACH if side == 0 else 0)
                    block = jnp.where(place == u, pltpu.roll(row, shift % COLS, 0), block)
                packed.append(block)
            packs[side, field] = jnp.concatenate(packed, 0).astype(bf16)
    span = 2 * REACH + 1
    basis_in[...] = jnp.zeros_like(basis_in)
    basis_in[: 3 * span * kernels, :rows] = m_ref[...].astype(f32)
    unit = lax.broadcasted_iota(jnp.int32, (16, 128), 0) == lax.broadcasted_iota(
        jnp.int32, (16, 128), 1
    )
    unit = jnp.where(unit, 1.0, 0.0).astype(bf16)
    for k in range(kernels):
        by_tap = basis_in[pl.ds(k, 16, stride=kernels), :].astype(bf16)
        flipped = mul(by_tap, unit, ((0,), (0,)))
        basis_by_row[pl.ds(k * rows, rows)] = flipped[:rows]
    lane = lax.broadcasted_iota(jnp.int32, (kernels, 128), 1)
    away = jnp.abs(lax.rem(lane, span) - REACH)
    by_row = [
        jnp.where(away <= reach_ref[i], basis_by_row[pl.ds(i, kernels, stride=rows), :], 0.0)
        for i in range(rows)
    ]
    rims[...] = jnp.where(north, by_row[-1], by_row[0])
    pl.semaphore_wait(barrier, n + 2)

    def push(src, dst, send, recv, to):
        copy = pltpu.make_async_remote_copy(
            src_ref=src, dst_ref=dst, send_sem=send, recv_sem=recv, device_id=to, device_id_type=MESH
        )
        copy.start()
        return copy

    pole_at = pl.multiple_of(lat * (points - 16), 16)
    edge_at = pl.multiple_of(other * (points - 16), 16)

    def send_field(field):
        edge = fc.at[field, pl.ds(edge_at, 16)]
        pole = fc.at[field, pl.ds(pole_at, 16)]
        copies = []
        for t in sorted(range(1, n), key=lambda t: -min(t, n - t)):
            copies.append(
                push(
                    pole, polar.at[field, n - t],
                    send_polar.at[field, t], recv_polar.at[field, n - t], (lat, turn(t)),
                )
            )
        routes = (
            (packs.at[0, field], sides.at[0, field], (lat, turn(1))),
            (packs.at[1, field], sides.at[1, field], (lat, turn(n - 1))),
            (edge, below.at[field, 0], (other, turn(1))),
            (edge, below.at[field, 2], (other, turn(n - 1))),
            (edge, below.at[field, 1], (other, lon)),
        )
        for r, (src, dst, to) in enumerate(routes):
            copies.append(push(src, dst, send_misc.at[field, r], recv_misc.at[field, r], to))
        polar[field, 0] = fc[field, pl.ds(pole_at, 16)]
        return copies

    field_copies = send_field(0)
    loads[3].wait()
    loads[4].wait()
    mat = jnp.concatenate(by_row, 0)
    taps_f[...] = mul(mat[:, :16].astype(bf16), d_ref[:, :lanes]).astype(bf16).astype(f32)
    zonal = [
        [h_ref[pl.ds(lat * 4 + a * 2 + r, kernels, stride=8), :] for r in range(2)] for a in range(2)
    ]
    rolled = [
        jnp.concatenate([pltpu.roll(z, j, 1) if j else z for z in zonal[a]], 1)
        for a in range(2)
        for j in range(COLS)
    ]
    high, low = split(jnp.concatenate(rolled, 0))

    def extend(field):
        gathered = polar[field].astype(f32).reshape(n, 2, COLS, channels)
        pole_rows = [gathered[:, r].reshape(n * COLS, channels) for r in range(2)]
        zeros = jnp.zeros((COLS, channels), f32)
        left, right = sides[0, field].astype(f32), sides[1, field].astype(f32)
        cells = fc[field].astype(f32)
        for i in range(rows):
            g, u = i // group, i % group
            ends = [side[COLS * g : COLS * (g + 1)] for side in (left, right)]
            line = [
                pltpu.roll(ends[0], (COLS - REACH - REACH * u) % COLS, 0),
                cells[COLS * i : COLS * (i + 1)],
                pltpu.roll(ends[1], (COLS - REACH * u) % COLS, 0),
                zeros,
            ]
            ext[field, pl.ds((i + 1) * SLOTS, SLOTS)] = jnp.concatenate(line, 0).astype(bf16)
        turned = gathered[n // 2 - 1 : n // 2 + 2]
        turned = jnp.where(north, turned[:, 0], turned[:, 1])
        beside = below[field].astype(f32).reshape(3, 2, COLS, channels)
        beside = jnp.where(north, beside[:, 0], beside[:, 1])
        top = jnp.where(north, turned, beside).reshape(3 * COLS, channels)
        bottom = jnp.where(north, beside, turned).reshape(3 * COLS, channels)
        ext[field, pl.ds(0, SLOTS)] = jnp.concatenate([top, zeros], 0).astype(bf16)
        ext[field, pl.ds((rows + 1) * SLOTS, SLOTS)] = jnp.concatenate([bottom, zeros], 0).astype(bf16)
        return jnp.concatenate(pole_rows, 0).astype(bf16)

    flip = lax.broadcasted_iota(jnp.int32, (128, 128), 0) + lax.broadcasted_iota(
        jnp.int32, (128, 128), 1
    )
    flip = jnp.where(flip == 127, 1.0, 0.0).astype(bf16)
    flip_high, flip_low = split(h_ref[...])
    rev[...] = mul(flip_high, flip) + mul(flip_low, flip)
    for r in range(2):
        turned = [
            rev[pl.ds(lat * 4 + a * 2 + r, kernels, stride=8), :] for a in range(2)
        ]
        for j in range(COLS):
            for a in range(2):
                circ[a, pl.ds((r * COLS + j) * kernels, kernels)] = pltpu.roll(turned[a], j + 1, 1)
    for copy in field_copies:
        copy.wait()
    cotangent_copies = send_field(1)
    cotangent_copies.append(push(rims, near, send_misc.at[0, 5], recv_misc.at[0, 5], (other, lon)))
    poles = extend(0)
    polar_part = mul(high, poles) + mul(low, poles)
    for p in range(pairs):
        taps = [
            taps_f[kernels * (2 * p + x // COLS) : kernels * (2 * p + x // COLS + 1),
                   x * window : (x + 1) * window]
            for x in range(16)
        ]
        taps = jnp.concatenate(taps, 0).astype(bf16)
        value = mul(taps, ext[0, pl.ds(2 * p * SLOTS, window)])
        if p == 0:
            value = value + jnp.where(north, polar_part, 0.0)
        if p == pairs - 1:
            value = value + jnp.where(north, 0.0, polar_part)
        for h in range(channels // 128):
            sums[h, pl.ds(16 * kernels * p, 16 * kernels)] = value[:, 128 * h : 128 * (h + 1)]

    cot = fc[1]

    def gradient(k):
        cells = [sums[h, pl.ds(k, points, stride=kernels), :] for h in range(channels // 128)]
        return mul(jnp.concatenate(cells, 1).astype(bf16), cot, ((0,), (0,)))

    line, spot = lon // GROUP, lax.rem(lon, GROUP)

    def in_plane(t):
        return (lat, line * GROUP + lax.rem(spot + t, GROUP))

    def on_line(t):
        return (lat, lax.rem(line + t, lines) * GROUP + spot)

    def rows_of(line_at, spot_at):
        return pl.ds(pl.multiple_of((line_at * GROUP + spot_at) * chunk, chunk), chunk)

    order = list(range(1, lines)) + [0]
    to_sib = {}
    for t in order:
        j = lax.rem(line + t, lines)
        sib_out[t] = gradient(other * half_k + j).astype(bf16)
        to_sib[t] = push(sib_out.at[t], sib_in.at[t], send_sib.at[t], recv_sib.at[t], (other, lon))
    for t in order:
        own[t] = gradient(lat * half_k + lax.rem(line + t, lines))
    plane = {}
    for t in order:
        j = lax.rem(line + t, lines)
        to_sib[t].wait()
        part[pl.ds(pl.multiple_of(j * channels, channels), channels)] = (
            own[t] + sib_in[t].astype(f32)
        ).astype(bf16)
        plane[t] = [
            push(
                part.at[rows_of(j, lax.rem(spot + u, GROUP))], plane_terms.at[u, t],
                send_plane.at[u, t], recv_plane.at[u, t], in_plane(u),
            )
            for u in range(1, GROUP)
        ]
    taps_each = 3 * (2 * REACH + 1)
    step = 2 * (2 * REACH + 1)
    first_taps = lane < taps_each - step
    up = jnp.where(first_taps, by_row[0], 0.0)
    up = pltpu.roll(up, step, 1)
    down = pltpu.roll(by_row[-1], 128 - step, 1)
    down = jnp.where(first_taps, down, 0.0)
    cotangent_copies[-1].wait()
    beside = near[...]
    mat = jnp.concatenate(
        [jnp.where(north, up, beside)] + by_row + [jnp.where(north, beside, down)], 0
    )
    spread = mul(mat[:, :16].astype(bf16), d_ref[:, lanes:])
    part_of = lax.broadcasted_iota(jnp.int32, (kernels, window), 1) // SLOTS
    for p in range(pairs):
        for x in range(16):
            tile = jnp.zeros((kernels, window), f32)
            for q in range(4):
                i = kernels * (2 * p + q)
                tile = jnp.where(
                    part_of == q, spread[i : i + kernels, x * window : (x + 1) * window], tile
                )
            taps_b[pl.ds((16 * p + x) * kernels, kernels)] = tile
    along = {}
    for t in order:
        total = part[rows_of(lax.rem(line + t, lines), spot)].astype(f32)
        for u in range(1, GROUP):
            plane[t][u - 1].wait()
            total = total + plane_terms[u, t].astype(f32)
        if t:
            plane_sums[t] = total.astype(bf16)
            along[t] = push(
                plane_sums.at[t], line_terms.at[t], send_line.at[t], recv_line.at[t], on_line(t)
            )

    acc[...] = jnp.zeros_like(acc)
    for copy in cotangent_copies[:-1]:
        copy.wait()
    poles = extend(1)
    loads[5].wait()

    def per_kernel(k, pole_acc):
        weight = w_ref[k]
        grad = mul(ext[1], weight, ((1,), (1,))).astype(bf16)
        for p in range(pairs):
            taps = taps_b[pl.ds(16 * kernels * p + k, 16, stride=kernels), :].astype(bf16)
            acc[pl.ds(16 * p, 16)] += mul(taps, grad[2 * p * SLOTS : 2 * p * SLOTS + window])
        pole_grad = mul(poles, weight, ((1,), (1,))).astype(bf16)
        high, low = split(
            jnp.concatenate([circ[a, pl.ds(k, 16, stride=kernels), :] for a in range(2)], 1)
        )
        return pole_acc + mul(high, pole_grad) + mul(low, pole_grad)

    pole_acc = jnp.zeros((16, channels), f32)
    pole_acc = lax.fori_loop(0, 3, per_kernel, pole_acc)
    here = rows_of(line, spot)
    for t in range(1, lines):
        along[t].wait()
        total = total + line_terms[t].astype(f32)
    mine[...] = total.astype(bf16)
    gw_ref[here] = mine[...]

    def spread_plane(src, at, t):
        return [
            push(src, gw_ref.at[at], send_copy.at[u, t], recv_copy.at[u, t], in_plane(u))
            for u in range(1, GROUP)
        ]

    near_first = sorted(range(1, lines), key=lambda t: min(t, lines - t))
    first = {
        t: push(mine, gw_ref.at[here], send_first.at[t], recv_first.at[t], on_line(t))
        for t in near_first
    }
    gather = spread_plane(mine, here, 0)
    done = 3
    for t in near_first:
        pole_acc = per_kernel(done, pole_acc)
        done += 1
        first[t].wait()
        at = rows_of(lax.rem(line - t + lines, lines), spot)
        gather += spread_plane(gw_ref.at[at], at, t)
    pole_acc = lax.fori_loop(done, kernels, per_kernel, pole_acc)
    acc[pl.ds(0, 16)] += jnp.where(north, pole_acc, 0.0)
    acc[pl.ds(points - 16, 16)] += jnp.where(north, 0.0, pole_acc)
    gf_ref[...] = acc[...].astype(bf16)
    for copy in gather:
        copy.wait()


def in_kernel(features, cotangent, weights, basis, polar_kernel, lon_reach):
    lat_rows, lon_cols, channels = features.shape
    kernels = weights.shape[0]
    n = lax.axis_size("lon")
    pairs, points = lat_rows // 2, lat_rows * lon_cols
    taps = 3 * (2 * REACH + 1)
    bf16, f32 = jnp.bfloat16, jnp.float32
    masked = basis.transpose(2, 3, 0, 1).reshape(taps * kernels, lat_rows)
    spread = jnp.asarray(spread_matrices(), bf16)
    half = kernels * channels // 2
    window, pack = 4 * SLOTS, lat_rows * REACH
    dma = pltpu.SemaphoreType.DMA
    vmem = pl.BlockSpec(memory_space=pltpu.VMEM)
    hbm = pl.BlockSpec(memory_space=pltpu.HBM)
    lines = n // GROUP
    grad_features, grad_weights = pl.pallas_call(
        functools.partial(fused, n),
        out_shape=(
            jax.ShapeDtypeStruct((points, channels), bf16),
            jax.ShapeDtypeStruct((half, channels), bf16),
        ),
        in_specs=[hbm] * 4 + [pl.BlockSpec(memory_space=pltpu.SMEM)] + [hbm] * 2,
        out_specs=(vmem, vmem),
        scratch_shapes=[
            pltpu.VMEM(weights.shape, bf16),
            pltpu.VMEM(masked.shape, bf16),
            pltpu.VMEM((kernels * 8, lon_cols * n), f32),
            pltpu.VMEM(spread.shape, bf16),
            dma((6,)),
            pltpu.VMEM((16 * kernels, 128), f32),
            pltpu.VMEM((kernels * lat_rows, 128), f32),
            pltpu.VMEM((2, points, channels), bf16),
            pltpu.VMEM((2, n, 16, channels), bf16),
            pltpu.VMEM((2, 2, pack, channels), bf16),
            pltpu.VMEM((2, 2, pack, channels), bf16),
            pltpu.VMEM((2, 3, 16, channels), bf16),
            pltpu.VMEM((kernels, 128), f32),
            pltpu.VMEM((kernels, 128), f32),
            pltpu.VMEM((lat_rows * kernels, 16 * window), f32),
            pltpu.VMEM((pairs * 16 * kernels, window), f32),
            pltpu.VMEM((kernels * 8, 128), f32),
            pltpu.VMEM((2, 16 * kernels, lon_cols * n), f32),
            pltpu.VMEM((2, (lat_rows + 2) * SLOTS, channels), bf16),
            pltpu.VMEM((channels // 128, points * kernels, 128), f32),
            pltpu.VMEM((lines, channels, channels), f32),
            pltpu.VMEM((lines, channels, channels), bf16),
            pltpu.VMEM((lines, channels, channels), bf16),
            pltpu.VMEM((half, channels), bf16),
            pltpu.VMEM((GROUP, lines, half // n, channels), bf16),
            pltpu.VMEM((lines, half // n, channels), bf16),
            pltpu.VMEM((lines, half // n, channels), bf16),
            pltpu.VMEM((half // n, channels), bf16),
            pltpu.VMEM((points, channels), f32),
            dma((2, n)), dma((2, n)), dma((2, 6)), dma((2, 6)), dma((4,)), dma((4,)),
            dma((GROUP, lines)), dma((GROUP, lines)), dma((lines,)), dma((lines,)),
            dma((GROUP, lines)), dma((GROUP, lines)), dma((lines,)), dma((lines,)),
        ],
        compiler_params=pltpu.CompilerParams(
            collective_id=0, has_side_effects=True, vmem_limit_bytes=56 * 2**20
        ),
    )(
        features.reshape(points, channels), cotangent.reshape(points, channels),
        weights, masked, lon_reach, polar_kernel.reshape(kernels * 8, lon_cols * n), spread,
    )
    return (
        grad_features.reshape(features.shape),
        grad_weights.astype(f32).reshape(kernels // 2, channels, channels),
    )


def choose(features, cotangent, weights, basis, polar_kernel, lon_reach):
    rows, cols, channels = features.shape
    n = lax.axis_size("lon")
    kernels = weights.shape[0]
    fits = (
        lax.axis_size("lat") == 2 and cols == COLS and n * COLS == 128 and n == GROUP * (kernels // 2) and rows % 8 == 0
        and kernels == 8 and (kernels // 2 * channels) % (16 * n) == 0
    )
    plan = in_kernel if fits else on_device
    return plan(features, cotangent, weights, basis, polar_kernel, lon_reach)


def solution(mesh):
    in_specs = (
        P("lat", "lon", None),
        P("lat", "lon", None),
        P(),
        P(None, "lat", None, None),
        P(),
        P("lat"),
    )
    out_specs = (P("lat", "lon", None), P("lat", None, None))
    return jax.shard_map(
        choose, mesh=mesh, in_specs=in_specs, out_specs=out_specs, check_vma=False
    )
```

```python
import functools

import jax
import jax.numpy as jnp
import numpy as np
from jax import lax
from jax.experimental import pallas as pl
from jax.experimental.pallas import tpu as pltpu
from jax.sharding import PartitionSpec as P

RADIUS = 1
REACH = 2
POLAR = 2


def padded(cells, sides, width, closed):
    for axis, dim in sides:
        count = lax.axis_size(axis)
        ends = count if closed else count - 1
        head = lax.slice_in_dim(cells, 0, width, axis=dim)
        tail = lax.slice_in_dim(cells, cells.shape[dim] - width, cells.shape[dim], axis=dim)
        cells = jnp.concatenate(
            [
                lax.ppermute(tail, axis, [(i, (i + 1) % count) for i in range(ends)]),
                cells,
                lax.ppermute(head, axis, [((i + 1) % count, i) for i in range(ends)]),
            ],
            axis=dim,
        )
    return cells


def from_behind(block, axis, distance):
    devices = range(lax.axis_size(axis))
    route = [((i - distance) % len(devices), i) for i in devices]
    return lax.ppermute(block, axis, route)


def on_device(features, cotangent, weights, basis, polar_kernel, lon_reach):
    lat_rows, lon_cols, channels = features.shape
    kernels = weights.shape[0]
    lat_count = lax.axis_size("lat")
    lon_count = lax.axis_size("lon")
    lat_index = lax.axis_index("lat")
    lon_index = lax.axis_index("lon")
    at_north = lat_index == 0
    at_south = lat_index == lat_count - 1
    at_pole = jnp.logical_or(at_north, at_south)
    lon_total = lon_cols * lon_count
    own_cols = lon_index * lon_cols + jnp.arange(lon_cols, dtype=jnp.int32)
    offsets = jnp.abs(jnp.arange(2 * REACH + 1, dtype=jnp.int32) - REACH)
    reach_mask = (offsets[None, :] <= lon_reach[:, None]).astype(basis.dtype)
    masked = basis * reach_mask[None, :, None, :]
    neighbours = padded(features, (("lat", 0),), RADIUS, False)
    partner_rows = from_behind(
        (features[:RADIUS], features[lat_rows - RADIUS :]), "lon", lon_count // 2
    )
    upper_rows = jnp.where(at_north, partner_rows[0][::-1], neighbours[:RADIUS])
    lower_rows = jnp.where(at_south, partner_rows[1][::-1], neighbours[lat_rows + RADIUS :])
    lengthened = jnp.concatenate([upper_rows, features, lower_rows], 0)
    widened = padded(lengthened, (("lon", 1),), REACH, True)
    basis_sum = jnp.zeros((kernels, lat_rows, lon_cols, channels), jnp.float32)
    for row_off in range(2 * RADIUS + 1):
        windows = jnp.stack(
            [
                widened[row_off : row_off + lat_rows, col_off : col_off + lon_cols]
                for col_off in range(2 * REACH + 1)
            ],
            1,
        )
        basis_sum = basis_sum + jnp.einsum(
            "kib,ibjc->kijc", masked[:, :, row_off], windows, preferred_element_type=jnp.float32
        )
    hemisphere = jnp.where(at_north, polar_kernel[:, 0], polar_kernel[:, 1])
    polar_in = jnp.where(at_north, features[:POLAR], features[lat_rows - POLAR :])
    polar_zero = jnp.zeros((kernels, POLAR, lon_cols, channels), jnp.float32)
    block_rows = lax.all_gather(polar_in, "lon", axis=1, tiled=True)

    def compute():
        source = jnp.arange(block_rows.shape[1], dtype=jnp.int32)
        offset_idx = (source[:, None] - own_cols[None, :]) % lon_total
        circulant = jnp.take(hemisphere, offset_idx, axis=3)
        return jnp.einsum(
            "kabuj,buc->kajc",
            circulant,
            block_rows.astype(jnp.float32),
            precision=lax.Precision.HIGHEST,
        )

    polar_out = lax.cond(at_pole, compute, lambda: polar_zero)
    basis_sum = basis_sum.at[:, :POLAR].add(jnp.where(at_north, polar_out, 0.0))
    basis_sum = basis_sum.at[:, lat_rows - POLAR :].add(jnp.where(at_south, polar_out, 0.0))
    contracted = basis_sum.astype(jnp.bfloat16)
    band_grad = lax.psum_scatter(
        jnp.einsum("kijc,ijo->kco", contracted, cotangent, preferred_element_type=jnp.float32),
        "lat",
        scatter_dimension=0,
        tiled=True,
    )
    grad_weights = lax.psum(band_grad, "lon")
    grad_basis = jnp.einsum(
        "kco,ijo->kijc", weights, cotangent, preferred_element_type=jnp.float32
    ).astype(jnp.bfloat16)
    grad_wide = jnp.zeros((lat_rows + 2 * RADIUS, lon_cols + 2 * REACH, channels), jnp.float32)
    for row_off in range(2 * RADIUS + 1):
        grad_win = jnp.einsum(
            "kib,kijc->ibjc", masked[:, :, row_off], grad_basis, preferred_element_type=jnp.float32
        )
        for col_off in range(2 * REACH + 1):
            grad_wide = grad_wide.at[
                row_off : row_off + lat_rows, col_off : col_off + lon_cols
            ].add(grad_win[:, col_off])
    lon_rims = jnp.concatenate([grad_wide[:, :REACH], grad_wide[:, lon_cols + REACH :]], 1)
    beside_all = padded(lon_rims, (("lon", 1),), REACH, True)
    folded = grad_wide[:, REACH : lon_cols + REACH]
    folded = folded.at[:, :REACH].add(beside_all[:, :REACH])
    folded = folded.at[:, lon_cols - REACH :].add(beside_all[:, 3 * REACH :])
    ghosts = jnp.concatenate([folded[:RADIUS], folded[lat_rows + RADIUS :]], 0)
    beside = padded(ghosts, (("lat", 0),), RADIUS, False)
    turned = from_behind((folded[:RADIUS], folded[lat_rows + RADIUS :]), "lon", lon_count // 2)
    interior = folded[RADIUS : lat_rows + RADIUS]
    from_above = jnp.where(at_north, turned[0][::-1], beside[:RADIUS])
    from_below = jnp.where(at_south, turned[1][::-1], beside[3 * RADIUS :])
    interior = interior.at[:RADIUS].add(from_above)
    interior = interior.at[lat_rows - RADIUS :].add(from_below)
    polar_cot = jnp.where(at_north, cotangent[:POLAR], cotangent[lat_rows - POLAR :])
    running = jnp.zeros((POLAR, lon_cols, channels), jnp.float32)
    add_block_rows = lax.all_gather(polar_cot, "lon", axis=1, tiled=True)

    def compute():
        source = jnp.arange(add_block_rows.shape[1], dtype=jnp.int32)
        offset_idx = (own_cols[None, :] - source[:, None]) % lon_total
        circulant = jnp.take(hemisphere, offset_idx, axis=3)
        block_grad = jnp.einsum(
            "kco,auo->kauc", weights, add_block_rows, preferred_element_type=jnp.float32
        ).astype(jnp.bfloat16)
        return jnp.einsum(
            "kabuj,kauc->bjc",
            circulant,
            block_grad.astype(jnp.float32),
            precision=lax.Precision.HIGHEST,
        )

    polar_grad = lax.cond(at_pole, compute, lambda: running)
    interior = interior.at[:POLAR].add(jnp.where(at_north, polar_grad, 0.0))
    interior = interior.at[lat_rows - POLAR :].add(jnp.where(at_south, polar_grad, 0.0))
    return (interior.astype(jnp.bfloat16), grad_weights)


GROUP = 4
COLS = 8
SLOTS = 32
MESH = pl.DeviceIdType.MESH


def spread_matrices():
    taps = 2 * REACH + 1
    forward = np.zeros((16, 2, COLS, 4, SLOTS), np.float32)
    backward = np.zeros((16, 2, COLS, 4, SLOTS), np.float32)
    for inner in range(2):
        for col in range(COLS):
            for row in range(4):
                for slot in range(SLOTS):
                    a, b = row - inner, slot - COLS - col + REACH
                    if 0 <= a < 3 and 0 <= b < taps:
                        forward[a * taps + b, inner, col, row, slot] = 1
                    a, b = inner - row + 2, col + REACH - (slot - COLS)
                    if 0 <= a < 3 and 0 <= b < taps:
                        backward[a * taps + b, inner, col, row, slot] = 1
    return np.concatenate([forward.reshape(16, -1), backward.reshape(16, -1)], 1)


def split(values):
    high = values.astype(jnp.bfloat16)
    return high, (values - high.astype(jnp.float32)).astype(jnp.bfloat16)


def mul(a, b, dims=((1,), (0,))):
    return lax.dot_general(a, b, (dims, ((), ())), preferred_element_type=jnp.float32)


def fused(
    n, f_hbm, c_hbm, w_hbm, m_hbm, reach_ref, h_hbm, d_hbm, gf_ref, gw_ref,
    w_ref, m_ref, h_ref, d_ref, load_sem, basis_in, basis_by_row,
    fc, polar, packs, sides, below, rims, near, taps_f, taps_b, rev, circ, ext, sums, own,
    sib_out, sib_in, part, plane_terms, plane_sums, line_terms, mine, acc,
    send_polar, recv_polar, send_misc, recv_misc, send_sib, recv_sib,
    send_plane, recv_plane, send_line, recv_line,
    send_copy, recv_copy, send_first, recv_first,
):
    f32, bf16 = jnp.float32, jnp.bfloat16
    lat, lon = lax.axis_index("lat"), lax.axis_index("lon")
    points, channels = f_hbm.shape
    rows = points // COLS
    pairs = rows // 2
    kernels = w_ref.shape[0]
    lines = n // GROUP
    half_k = kernels // 2
    chunk = half_k * channels // n
    window = 4 * SLOTS
    lanes = 16 * window
    other = 1 - lat
    north = lat == 0

    def turn(t):
        return lax.rem(lon + t, n)

    barrier = pltpu.get_barrier_semaphore()
    for t in range(1, n):
        pl.semaphore_signal(barrier, inc=1, device_id=(lat, turn(t)), device_id_type=MESH)
    for t in (0, 1, n - 1):
        pl.semaphore_signal(barrier, inc=1, device_id=(other, turn(t)), device_id_type=MESH)

    sources = (f_hbm, c_hbm, m_hbm, d_hbm, h_hbm, w_hbm)
    places = (fc.at[0], fc.at[1], m_ref, d_ref, h_ref, w_ref)
    loads = [
        pltpu.make_async_copy(src, dst, load_sem.at[i])
        for i, (src, dst) in enumerate(zip(sources, places))
    ]
    for load in loads:
        load.start()
    for load in loads[:3]:
        load.wait()
    place = lax.broadcasted_iota(jnp.int32, (COLS, channels), 0) // REACH
    group = COLS // REACH
    for field in range(2):
        cells = fc[field].astype(f32)
        for side in range(2):
            packed = []
            for g in range(rows // group):
                block = jnp.zeros((COLS, channels), f32)
                for u in range(group):
                    row = cells[COLS * (group * g + u) : COLS * (group * g + u + 1)]
                    shift = REACH * u + (REACH if side == 0 else 0)
                    block = jnp.where(place == u, pltpu.roll(row, shift % COLS, 0), block)
                packed.append(block)
            packs[side, field] = jnp.concatenate(packed, 0).astype(bf16)
    span = 2 * REACH + 1
    basis_in[...] = jnp.zeros_like(basis_in)
    basis_in[: 3 * span * kernels, :rows] = m_ref[...].astype(f32)
    unit = lax.broadcasted_iota(jnp.int32, (16, 128), 0) == lax.broadcasted_iota(
        jnp.int32, (16, 128), 1
    )
    unit = jnp.where(unit, 1.0, 0.0).astype(bf16)
    for k in range(kernels):
        by_tap = basis_in[pl.ds(k, 16, stride=kernels), :].astype(bf16)
        flipped = mul(by_tap, unit, ((0,), (0,)))
        basis_by_row[pl.ds(k * rows, rows)] = flipped[:rows]
    lane = lax.broadcasted_iota(jnp.int32, (kernels, 128), 1)
    away = jnp.abs(lax.rem(lane, span) - REACH)
    by_row = [
        jnp.where(away <= reach_ref[i], basis_by_row[pl.ds(i, kernels, stride=rows), :], 0.0)
        for i in range(rows)
    ]
    rims[...] = jnp.where(north, by_row[-1], by_row[0])
    pl.semaphore_wait(barrier, n + 2)

    def push(src, dst, send, recv, to):
        copy = pltpu.make_async_remote_copy(
            src_ref=src, dst_ref=dst, send_sem=send, recv_sem=recv, device_id=to, device_id_type=MESH
        )
        copy.start()
        return copy

    pole_at = pl.multiple_of(lat * (points - 16), 16)
    edge_at = pl.multiple_of(other * (points - 16), 16)

    def send_field(field):
        edge = fc.at[field, pl.ds(edge_at, 16)]
        pole = fc.at[field, pl.ds(pole_at, 16)]
        copies = []
        for t in sorted(range(1, n), key=lambda t: -min(t, n - t)):
            copies.append(
                push(
                    pole, polar.at[field, n - t],
                    send_polar.at[field, t], recv_polar.at[field, n - t], (lat, turn(t)),
                )
            )
        routes = (
            (packs.at[0, field], sides.at[0, field], (lat, turn(1))),
            (packs.at[1, field], sides.at[1, field], (lat, turn(n - 1))),
            (edge, below.at[field, 0], (other, turn(1))),
            (edge, below.at[field, 2], (other, turn(n - 1))),
            (edge, below.at[field, 1], (other, lon)),
        )
        for r, (src, dst, to) in enumerate(routes):
            copies.append(push(src, dst, send_misc.at[field, r], recv_misc.at[field, r], to))
        polar[field, 0] = fc[field, pl.ds(pole_at, 16)]
        return copies

    field_copies = send_field(0)
    loads[3].wait()
    loads[4].wait()
    mat = jnp.concatenate(by_row, 0)
    taps_f[...] = mul(mat[:, :16].astype(bf16), d_ref[:, :lanes]).astype(bf16).astype(f32)
    zonal = [
        [h_ref[pl.ds(lat * 4 + a * 2 + r, kernels, stride=8), :] for r in range(2)] for a in range(2)
    ]
    rolled = [
        jnp.concatenate([pltpu.roll(z, j, 1) if j else z for z in zonal[a]], 1)
        for a in range(2)
        for j in range(COLS)
    ]
    high, low = split(jnp.concatenate(rolled, 0))

    def extend(field):
        gathered = polar[field].astype(f32).reshape(n, 2, COLS, channels)
        pole_rows = [gathered[:, r].reshape(n * COLS, channels) for r in range(2)]
        zeros = jnp.zeros((COLS, channels), f32)
        left, right = sides[0, field].astype(f32), sides[1, field].astype(f32)
        cells = fc[field].astype(f32)
        for i in range(rows):
            g, u = i // group, i % group
            ends = [side[COLS * g : COLS * (g + 1)] for side in (left, right)]
            line = [
                pltpu.roll(ends[0], (COLS - REACH - REACH * u) % COLS, 0),
                cells[COLS * i : COLS * (i + 1)],
                pltpu.roll(ends[1], (COLS - REACH * u) % COLS, 0),
                zeros,
            ]
            ext[field, pl.ds((i + 1) * SLOTS, SLOTS)] = jnp.concatenate(line, 0).astype(bf16)
        turned = gathered[n // 2 - 1 : n // 2 + 2]
        turned = jnp.where(north, turned[:, 0], turned[:, 1])
        beside = below[field].astype(f32).reshape(3, 2, COLS, channels)
        beside = jnp.where(north, beside[:, 0], beside[:, 1])
        top = jnp.where(north, turned, beside).reshape(3 * COLS, channels)
        bottom = jnp.where(north, beside, turned).reshape(3 * COLS, channels)
        ext[field, pl.ds(0, SLOTS)] = jnp.concatenate([top, zeros], 0).astype(bf16)
        ext[field, pl.ds((rows + 1) * SLOTS, SLOTS)] = jnp.concatenate([bottom, zeros], 0).astype(bf16)
        return jnp.concatenate(pole_rows, 0).astype(bf16)

    flip = lax.broadcasted_iota(jnp.int32, (128, 128), 0) + lax.broadcasted_iota(
        jnp.int32, (128, 128), 1
    )
    flip = jnp.where(flip == 127, 1.0, 0.0).astype(bf16)
    flip_high, flip_low = split(h_ref[...])
    rev[...] = mul(flip_high, flip) + mul(flip_low, flip)
    for r in range(2):
        turned = [
            rev[pl.ds(lat * 4 + a * 2 + r, kernels, stride=8), :] for a in range(2)
        ]
        for j in range(COLS):
            for a in range(2):
                circ[a, pl.ds((r * COLS + j) * kernels, kernels)] = pltpu.roll(turned[a], j + 1, 1)
    for copy in field_copies:
        copy.wait()
    cotangent_copies = send_field(1)
    cotangent_copies.append(push(rims, near, send_misc.at[0, 5], recv_misc.at[0, 5], (other, lon)))
    poles = extend(0)
    polar_part = mul(high, poles) + mul(low, poles)
    for p in range(pairs):
        taps = [
            taps_f[kernels * (2 * p + x // COLS) : kernels * (2 * p + x // COLS + 1),
                   x * window : (x + 1) * window]
            for x in range(16)
        ]
        taps = jnp.concatenate(taps, 0).astype(bf16)
        value = mul(taps, ext[0, pl.ds(2 * p * SLOTS, window)])
        if p == 0:
            value = value + jnp.where(north, polar_part, 0.0)
        if p == pairs - 1:
            value = value + jnp.where(north, 0.0, polar_part)
        for h in range(channels // 128):
            sums[h, pl.ds(16 * kernels * p, 16 * kernels)] = value[:, 128 * h : 128 * (h + 1)]

    cot = fc[1]

    def gradient(k):
        cells = [sums[h, pl.ds(k, points, stride=kernels), :] for h in range(channels // 128)]
        return mul(jnp.concatenate(cells, 1).astype(bf16), cot, ((0,), (0,)))

    line, spot = lon // GROUP, lax.rem(lon, GROUP)

    def in_plane(t):
        return (lat, line * GROUP + lax.rem(spot + t, GROUP))

    def on_line(t):
        return (lat, lax.rem(line + t, lines) * GROUP + spot)

    def rows_of(line_at, spot_at):
        return pl.ds(pl.multiple_of((line_at * GROUP + spot_at) * chunk, chunk), chunk)

    order = list(range(1, lines)) + [0]
    to_sib = {}
    for t in order:
        j = lax.rem(line + t, lines)
        sib_out[t] = gradient(other * half_k + j).astype(bf16)
        to_sib[t] = push(sib_out.at[t], sib_in.at[t], send_sib.at[t], recv_sib.at[t], (other, lon))
    for t in order:
        own[t] = gradient(lat * half_k + lax.rem(line + t, lines))
    plane = {}
    for t in order:
        j = lax.rem(line + t, lines)
        to_sib[t].wait()
        part[pl.ds(pl.multiple_of(j * channels, channels), channels)] = (
            own[t] + sib_in[t].astype(f32)
        ).astype(bf16)
        plane[t] = [
            push(
                part.at[rows_of(j, lax.rem(spot + u, GROUP))], plane_terms.at[u, t],
                send_plane.at[u, t], recv_plane.at[u, t], in_plane(u),
            )
            for u in range(1, GROUP)
        ]
    taps_each = 3 * (2 * REACH + 1)
    step = 2 * (2 * REACH + 1)
    first_taps = lane < taps_each - step
    up = jnp.where(first_taps, by_row[0], 0.0)
    up = pltpu.roll(up, step, 1)
    down = pltpu.roll(by_row[-1], 128 - step, 1)
    down = jnp.where(first_taps, down, 0.0)
    cotangent_copies[-1].wait()
    beside = near[...]
    mat = jnp.concatenate(
        [jnp.where(north, up, beside)] + by_row + [jnp.where(north, beside, down)], 0
    )
    spread = mul(mat[:, :16].astype(bf16), d_ref[:, lanes:])
    part_of = lax.broadcasted_iota(jnp.int32, (kernels, window), 1) // SLOTS
    for p in range(pairs):
        for x in range(16):
            tile = jnp.zeros((kernels, window), f32)
            for q in range(4):
                i = kernels * (2 * p + q)
                tile = jnp.where(
                    part_of == q, spread[i : i + kernels, x * window : (x + 1) * window], tile
                )
            taps_b[pl.ds((16 * p + x) * kernels, kernels)] = tile
    along = {}
    for t in order:
        total = part[rows_of(lax.rem(line + t, lines), spot)].astype(f32)
        for u in range(1, GROUP):
            plane[t][u - 1].wait()
            total = total + plane_terms[u, t].astype(f32)
        if t:
            plane_sums[t] = total.astype(bf16)
            along[t] = push(
                plane_sums.at[t], line_terms.at[t], send_line.at[t], recv_line.at[t], on_line(t)
            )

    acc[...] = jnp.zeros_like(acc)
    for copy in cotangent_copies[:-1]:
        copy.wait()
    poles = extend(1)
    loads[5].wait()

    def per_kernel(k, pole_acc):
        weight = w_ref[k]
        grad = mul(ext[1], weight, ((1,), (1,))).astype(bf16)
        for p in range(pairs):
            taps = taps_b[pl.ds(16 * kernels * p + k, 16, stride=kernels), :].astype(bf16)
            acc[pl.ds(16 * p, 16)] += mul(taps, grad[2 * p * SLOTS : 2 * p * SLOTS + window])
        pole_grad = mul(poles, weight, ((1,), (1,))).astype(bf16)
        high, low = split(
            jnp.concatenate([circ[a, pl.ds(k, 16, stride=kernels), :] for a in range(2)], 1)
        )
        return pole_acc + mul(high, pole_grad) + mul(low, pole_grad)

    pole_acc = jnp.zeros((16, channels), f32)
    pole_acc = lax.fori_loop(0, 1, per_kernel, pole_acc)
    here = rows_of(line, spot)
    for t in range(1, lines):
        along[t].wait()
        total = total + line_terms[t].astype(f32)
    mine[...] = total.astype(bf16)
    gw_ref[here] = mine[...]

    def spread_plane(src, at, t):
        return [
            push(src, gw_ref.at[at], send_copy.at[u, t], recv_copy.at[u, t], in_plane(u))
            for u in range(1, GROUP)
        ]

    near_first = sorted(range(1, lines), key=lambda t: min(t, lines - t))
    first = {
        t: push(mine, gw_ref.at[here], send_first.at[t], recv_first.at[t], on_line(t))
        for t in near_first
    }
    gather = spread_plane(mine, here, 0)
    done = 1
    for t in near_first:
        pole_acc = per_kernel(done, pole_acc)
        done += 1
        first[t].wait()
        at = rows_of(lax.rem(line - t + lines, lines), spot)
        gather += spread_plane(gw_ref.at[at], at, t)
    pole_acc = lax.fori_loop(done, kernels, per_kernel, pole_acc)
    acc[pl.ds(0, 16)] += jnp.where(north, pole_acc, 0.0)
    acc[pl.ds(points - 16, 16)] += jnp.where(north, 0.0, pole_acc)
    gf_ref[...] = acc[...].astype(bf16)
    for copy in gather:
        copy.wait()


def in_kernel(features, cotangent, weights, basis, polar_kernel, lon_reach):
    lat_rows, lon_cols, channels = features.shape
    kernels = weights.shape[0]
    n = lax.axis_size("lon")
    pairs, points = lat_rows // 2, lat_rows * lon_cols
    taps = 3 * (2 * REACH + 1)
    bf16, f32 = jnp.bfloat16, jnp.float32
    masked = basis.transpose(2, 3, 0, 1).reshape(taps * kernels, lat_rows)
    spread = jnp.asarray(spread_matrices(), bf16)
    half = kernels * channels // 2
    window, pack = 4 * SLOTS, lat_rows * REACH
    dma = pltpu.SemaphoreType.DMA
    vmem = pl.BlockSpec(memory_space=pltpu.VMEM)
    hbm = pl.BlockSpec(memory_space=pltpu.HBM)
    lines = n // GROUP
    grad_features, grad_weights = pl.pallas_call(
        functools.partial(fused, n),
        out_shape=(
            jax.ShapeDtypeStruct((points, channels), bf16),
            jax.ShapeDtypeStruct((half, channels), bf16),
        ),
        in_specs=[hbm] * 4 + [pl.BlockSpec(memory_space=pltpu.SMEM)] + [hbm] * 2,
        out_specs=(vmem, vmem),
        scratch_shapes=[
            pltpu.VMEM(weights.shape, bf16),
            pltpu.VMEM(masked.shape, bf16),
            pltpu.VMEM((kernels * 8, lon_cols * n), f32),
            pltpu.VMEM(spread.shape, bf16),
            dma((6,)),
            pltpu.VMEM((16 * kernels, 128), f32),
            pltpu.VMEM((kernels * lat_rows, 128), f32),
            pltpu.VMEM((2, points, channels), bf16),
            pltpu.VMEM((2, n, 16, channels), bf16),
            pltpu.VMEM((2, 2, pack, channels), bf16),
            pltpu.VMEM((2, 2, pack, channels), bf16),
            pltpu.VMEM((2, 3, 16, channels), bf16),
            pltpu.VMEM((kernels, 128), f32),
            pltpu.VMEM((kernels, 128), f32),
            pltpu.VMEM((lat_rows * kernels, 16 * window), f32),
            pltpu.VMEM((pairs * 16 * kernels, window), f32),
            pltpu.VMEM((kernels * 8, 128), f32),
            pltpu.VMEM((2, 16 * kernels, lon_cols * n), f32),
            pltpu.VMEM((2, (lat_rows + 2) * SLOTS, channels), bf16),
            pltpu.VMEM((channels // 128, points * kernels, 128), f32),
            pltpu.VMEM((lines, channels, channels), f32),
            pltpu.VMEM((lines, channels, channels), bf16),
            pltpu.VMEM((lines, channels, channels), bf16),
            pltpu.VMEM((half, channels), bf16),
            pltpu.VMEM((GROUP, lines, half // n, channels), bf16),
            pltpu.VMEM((lines, half // n, channels), bf16),
            pltpu.VMEM((lines, half // n, channels), bf16),
            pltpu.VMEM((half // n, channels), bf16),
            pltpu.VMEM((points, channels), f32),
            dma((2, n)), dma((2, n)), dma((2, 6)), dma((2, 6)), dma((4,)), dma((4,)),
            dma((GROUP, lines)), dma((GROUP, lines)), dma((lines,)), dma((lines,)),
            dma((GROUP, lines)), dma((GROUP, lines)), dma((lines,)), dma((lines,)),
        ],
        compiler_params=pltpu.CompilerParams(
            collective_id=0, has_side_effects=True, vmem_limit_bytes=56 * 2**20
        ),
    )(
        features.reshape(points, channels), cotangent.reshape(points, channels),
        weights, masked, lon_reach, polar_kernel.reshape(kernels * 8, lon_cols * n), spread,
    )
    return (
        grad_features.reshape(features.shape),
        grad_weights.astype(f32).reshape(kernels // 2, channels, channels),
    )


def choose(features, cotangent, weights, basis, polar_kernel, lon_reach):
    rows, cols, channels = features.shape
    n = lax.axis_size("lon")
    kernels = weights.shape[0]
    fits = (
        lax.axis_size("lat") == 2 and cols == COLS and n * COLS == 128 and n == GROUP * (kernels // 2) and rows % 8 == 0
        and kernels == 8 and (kernels // 2 * channels) % (16 * n) == 0
    )
    plan = in_kernel if fits else on_device
    return plan(features, cotangent, weights, basis, polar_kernel, lon_reach)


def solution(mesh):
    in_specs = (
        P("lat", "lon", None),
        P("lat", "lon", None),
        P(),
        P(None, "lat", None, None),
        P(),
        P("lat"),
    )
    out_specs = (P("lat", "lon", None), P("lat", None, None))
    return jax.shard_map(
        choose, mesh=mesh, in_specs=in_specs, out_specs=out_specs, check_vma=False
    )
```

```python
import functools

import jax
import jax.numpy as jnp
import numpy as np
from jax import lax
from jax.experimental import pallas as pl
from jax.experimental.pallas import tpu as pltpu
from jax.sharding import PartitionSpec as P

RADIUS = 1
REACH = 2
POLAR = 2


def padded(cells, sides, width, closed):
    for axis, dim in sides:
        count = lax.axis_size(axis)
        ends = count if closed else count - 1
        head = lax.slice_in_dim(cells, 0, width, axis=dim)
        tail = lax.slice_in_dim(cells, cells.shape[dim] - width, cells.shape[dim], axis=dim)
        cells = jnp.concatenate(
            [
                lax.ppermute(tail, axis, [(i, (i + 1) % count) for i in range(ends)]),
                cells,
                lax.ppermute(head, axis, [((i + 1) % count, i) for i in range(ends)]),
            ],
            axis=dim,
        )
    return cells


def from_behind(block, axis, distance):
    devices = range(lax.axis_size(axis))
    route = [((i - distance) % len(devices), i) for i in devices]
    return lax.ppermute(block, axis, route)


def on_device(features, cotangent, weights, basis, polar_kernel, lon_reach):
    lat_rows, lon_cols, channels = features.shape
    kernels = weights.shape[0]
    lat_count = lax.axis_size("lat")
    lon_count = lax.axis_size("lon")
    lat_index = lax.axis_index("lat")
    lon_index = lax.axis_index("lon")
    at_north = lat_index == 0
    at_south = lat_index == lat_count - 1
    at_pole = jnp.logical_or(at_north, at_south)
    lon_total = lon_cols * lon_count
    own_cols = lon_index * lon_cols + jnp.arange(lon_cols, dtype=jnp.int32)
    offsets = jnp.abs(jnp.arange(2 * REACH + 1, dtype=jnp.int32) - REACH)
    reach_mask = (offsets[None, :] <= lon_reach[:, None]).astype(basis.dtype)
    masked = basis * reach_mask[None, :, None, :]
    neighbours = padded(features, (("lat", 0),), RADIUS, False)
    partner_rows = from_behind(
        (features[:RADIUS], features[lat_rows - RADIUS :]), "lon", lon_count // 2
    )
    upper_rows = jnp.where(at_north, partner_rows[0][::-1], neighbours[:RADIUS])
    lower_rows = jnp.where(at_south, partner_rows[1][::-1], neighbours[lat_rows + RADIUS :])
    lengthened = jnp.concatenate([upper_rows, features, lower_rows], 0)
    widened = padded(lengthened, (("lon", 1),), REACH, True)
    basis_sum = jnp.zeros((kernels, lat_rows, lon_cols, channels), jnp.float32)
    for row_off in range(2 * RADIUS + 1):
        windows = jnp.stack(
            [
                widened[row_off : row_off + lat_rows, col_off : col_off + lon_cols]
                for col_off in range(2 * REACH + 1)
            ],
            1,
        )
        basis_sum = basis_sum + jnp.einsum(
            "kib,ibjc->kijc", masked[:, :, row_off], windows, preferred_element_type=jnp.float32
        )
    hemisphere = jnp.where(at_north, polar_kernel[:, 0], polar_kernel[:, 1])
    polar_in = jnp.where(at_north, features[:POLAR], features[lat_rows - POLAR :])
    polar_zero = jnp.zeros((kernels, POLAR, lon_cols, channels), jnp.float32)
    block_rows = lax.all_gather(polar_in, "lon", axis=1, tiled=True)

    def compute():
        source = jnp.arange(block_rows.shape[1], dtype=jnp.int32)
        offset_idx = (source[:, None] - own_cols[None, :]) % lon_total
        circulant = jnp.take(hemisphere, offset_idx, axis=3)
        return jnp.einsum(
            "kabuj,buc->kajc",
            circulant,
            block_rows.astype(jnp.float32),
            precision=lax.Precision.HIGHEST,
        )

    polar_out = lax.cond(at_pole, compute, lambda: polar_zero)
    basis_sum = basis_sum.at[:, :POLAR].add(jnp.where(at_north, polar_out, 0.0))
    basis_sum = basis_sum.at[:, lat_rows - POLAR :].add(jnp.where(at_south, polar_out, 0.0))
    contracted = basis_sum.astype(jnp.bfloat16)
    band_grad = lax.psum_scatter(
        jnp.einsum("kijc,ijo->kco", contracted, cotangent, preferred_element_type=jnp.float32),
        "lat",
        scatter_dimension=0,
        tiled=True,
    )
    grad_weights = lax.psum(band_grad, "lon")
    grad_basis = jnp.einsum(
        "kco,ijo->kijc", weights, cotangent, preferred_element_type=jnp.float32
    ).astype(jnp.bfloat16)
    grad_wide = jnp.zeros((lat_rows + 2 * RADIUS, lon_cols + 2 * REACH, channels), jnp.float32)
    for row_off in range(2 * RADIUS + 1):
        grad_win = jnp.einsum(
            "kib,kijc->ibjc", masked[:, :, row_off], grad_basis, preferred_element_type=jnp.float32
        )
        for col_off in range(2 * REACH + 1):
            grad_wide = grad_wide.at[
                row_off : row_off + lat_rows, col_off : col_off + lon_cols
            ].add(grad_win[:, col_off])
    lon_rims = jnp.concatenate([grad_wide[:, :REACH], grad_wide[:, lon_cols + REACH :]], 1)
    beside_all = padded(lon_rims, (("lon", 1),), REACH, True)
    folded = grad_wide[:, REACH : lon_cols + REACH]
    folded = folded.at[:, :REACH].add(beside_all[:, :REACH])
    folded = folded.at[:, lon_cols - REACH :].add(beside_all[:, 3 * REACH :])
    ghosts = jnp.concatenate([folded[:RADIUS], folded[lat_rows + RADIUS :]], 0)
    beside = padded(ghosts, (("lat", 0),), RADIUS, False)
    turned = from_behind((folded[:RADIUS], folded[lat_rows + RADIUS :]), "lon", lon_count // 2)
    interior = folded[RADIUS : lat_rows + RADIUS]
    from_above = jnp.where(at_north, turned[0][::-1], beside[:RADIUS])
    from_below = jnp.where(at_south, turned[1][::-1], beside[3 * RADIUS :])
    interior = interior.at[:RADIUS].add(from_above)
    interior = interior.at[lat_rows - RADIUS :].add(from_below)
    polar_cot = jnp.where(at_north, cotangent[:POLAR], cotangent[lat_rows - POLAR :])
    running = jnp.zeros((POLAR, lon_cols, channels), jnp.float32)
    add_block_rows = lax.all_gather(polar_cot, "lon", axis=1, tiled=True)

    def compute():
        source = jnp.arange(add_block_rows.shape[1], dtype=jnp.int32)
        offset_idx = (own_cols[None, :] - source[:, None]) % lon_total
        circulant = jnp.take(hemisphere, offset_idx, axis=3)
        block_grad = jnp.einsum(
            "kco,auo->kauc", weights, add_block_rows, preferred_element_type=jnp.float32
        ).astype(jnp.bfloat16)
        return jnp.einsum(
            "kabuj,kauc->bjc",
            circulant,
            block_grad.astype(jnp.float32),
            precision=lax.Precision.HIGHEST,
        )

    polar_grad = lax.cond(at_pole, compute, lambda: running)
    interior = interior.at[:POLAR].add(jnp.where(at_north, polar_grad, 0.0))
    interior = interior.at[lat_rows - POLAR :].add(jnp.where(at_south, polar_grad, 0.0))
    return (interior.astype(jnp.bfloat16), grad_weights)


GROUP = 4
COLS = 8
SLOTS = 32
MESH = pl.DeviceIdType.MESH


def spread_matrices():
    taps = 2 * REACH + 1
    forward = np.zeros((16, 2, COLS, 4, SLOTS), np.float32)
    backward = np.zeros((16, 2, COLS, 4, SLOTS), np.float32)
    for inner in range(2):
        for col in range(COLS):
            for row in range(4):
                for slot in range(SLOTS):
                    a, b = row - inner, slot - COLS - col + REACH
                    if 0 <= a < 3 and 0 <= b < taps:
                        forward[a * taps + b, inner, col, row, slot] = 1
                    a, b = inner - row + 2, col + REACH - (slot - COLS)
                    if 0 <= a < 3 and 0 <= b < taps:
                        backward[a * taps + b, inner, col, row, slot] = 1
    return np.concatenate([forward.reshape(16, -1), backward.reshape(16, -1)], 1)


def split(values):
    high = values.astype(jnp.bfloat16)
    return high, (values - high.astype(jnp.float32)).astype(jnp.bfloat16)


def mul(a, b, dims=((1,), (0,))):
    return lax.dot_general(a, b, (dims, ((), ())), preferred_element_type=jnp.float32)


def fused(
    n, f_hbm, c_hbm, w_hbm, m_hbm, reach_ref, h_hbm, d_hbm, gf_ref, gw_ref,
    w_ref, m_ref, h_ref, d_ref, load_sem, basis_in, basis_by_row,
    fc, polar, packs, sides, below, rims, near, taps_f, taps_b, rev, circ, ext, sums, own,
    sib_out, sib_in, part, plane_terms, plane_sums, line_terms, mine, acc,
    send_polar, recv_polar, send_misc, recv_misc, send_sib, recv_sib,
    send_plane, recv_plane, send_line, recv_line,
    send_copy, recv_copy, send_first, recv_first,
):
    f32, bf16 = jnp.float32, jnp.bfloat16
    lat, lon = lax.axis_index("lat"), lax.axis_index("lon")
    points, channels = f_hbm.shape
    rows = points // COLS
    pairs = rows // 2
    kernels = w_ref.shape[0]
    lines = n // GROUP
    half_k = kernels // 2
    chunk = half_k * channels // n
    window = 4 * SLOTS
    lanes = 16 * window
    other = 1 - lat
    north = lat == 0

    def turn(t):
        return lax.rem(lon + t, n)

    barrier = pltpu.get_barrier_semaphore()
    for t in range(1, n):
        pl.semaphore_signal(barrier, inc=1, device_id=(lat, turn(t)), device_id_type=MESH)
    for t in (0, 1, n - 1):
        pl.semaphore_signal(barrier, inc=1, device_id=(other, turn(t)), device_id_type=MESH)

    sources = (f_hbm, c_hbm, m_hbm, d_hbm, h_hbm, w_hbm)
    places = (fc.at[0], fc.at[1], m_ref, d_ref, h_ref, w_ref)
    loads = [
        pltpu.make_async_copy(src, dst, load_sem.at[i])
        for i, (src, dst) in enumerate(zip(sources, places))
    ]
    for load in loads:
        load.start()
    for load in loads[:3]:
        load.wait()
    place = lax.broadcasted_iota(jnp.int32, (COLS, channels), 0) // REACH
    group = COLS // REACH
    for field in range(2):
        cells = fc[field].astype(f32)
        for side in range(2):
            packed = []
            for g in range(rows // group):
                block = jnp.zeros((COLS, channels), f32)
                for u in range(group):
                    row = cells[COLS * (group * g + u) : COLS * (group * g + u + 1)]
                    shift = REACH * u + (REACH if side == 0 else 0)
                    block = jnp.where(place == u, pltpu.roll(row, shift % COLS, 0), block)
                packed.append(block)
            packs[side, field] = jnp.concatenate(packed, 0).astype(bf16)
    span = 2 * REACH + 1
    basis_in[...] = jnp.zeros_like(basis_in)
    basis_in[: 3 * span * kernels, :rows] = m_ref[...].astype(f32)
    unit = lax.broadcasted_iota(jnp.int32, (16, 128), 0) == lax.broadcasted_iota(
        jnp.int32, (16, 128), 1
    )
    unit = jnp.where(unit, 1.0, 0.0).astype(bf16)
    for k in range(kernels):
        by_tap = basis_in[pl.ds(k, 16, stride=kernels), :].astype(bf16)
        flipped = mul(by_tap, unit, ((0,), (0,)))
        basis_by_row[pl.ds(k * rows, rows)] = flipped[:rows]
    lane = lax.broadcasted_iota(jnp.int32, (kernels, 128), 1)
    away = jnp.abs(lax.rem(lane, span) - REACH)
    by_row = [
        jnp.where(away <= reach_ref[i], basis_by_row[pl.ds(i, kernels, stride=rows), :], 0.0)
        for i in range(rows)
    ]
    rims[...] = jnp.where(north, by_row[-1], by_row[0])
    pl.semaphore_wait(barrier, n + 2)

    def push(src, dst, send, recv, to):
        copy = pltpu.make_async_remote_copy(
            src_ref=src, dst_ref=dst, send_sem=send, recv_sem=recv, device_id=to, device_id_type=MESH
        )
        copy.start()
        return copy

    pole_at = pl.multiple_of(lat * (points - 16), 16)
    edge_at = pl.multiple_of(other * (points - 16), 16)

    def send_field(field):
        edge = fc.at[field, pl.ds(edge_at, 16)]
        pole = fc.at[field, pl.ds(pole_at, 16)]
        copies = []
        for t in sorted(range(1, n), key=lambda t: -min(t, n - t)):
            copies.append(
                push(
                    pole, polar.at[field, n - t],
                    send_polar.at[field, t], recv_polar.at[field, n - t], (lat, turn(t)),
                )
            )
        routes = (
            (packs.at[0, field], sides.at[0, field], (lat, turn(1))),
            (packs.at[1, field], sides.at[1, field], (lat, turn(n - 1))),
            (edge, below.at[field, 0], (other, turn(1))),
            (edge, below.at[field, 2], (other, turn(n - 1))),
            (edge, below.at[field, 1], (other, lon)),
        )
        for r, (src, dst, to) in enumerate(routes):
            copies.append(push(src, dst, send_misc.at[field, r], recv_misc.at[field, r], to))
        polar[field, 0] = fc[field, pl.ds(pole_at, 16)]
        return copies

    field_copies = send_field(0)
    loads[3].wait()
    loads[4].wait()
    mat = jnp.concatenate(by_row, 0)
    taps_f[...] = mul(mat[:, :16].astype(bf16), d_ref[:, :lanes]).astype(bf16).astype(f32)
    zonal = [
        [h_ref[pl.ds(lat * 4 + a * 2 + r, kernels, stride=8), :] for r in range(2)] for a in range(2)
    ]
    rolled = [
        jnp.concatenate([pltpu.roll(z, j, 1) if j else z for z in zonal[a]], 1)
        for a in range(2)
        for j in range(COLS)
    ]
    high, low = split(jnp.concatenate(rolled, 0))

    def extend_inside(field):
        zeros = jnp.zeros((COLS, channels), f32)
        left, right = sides[0, field].astype(f32), sides[1, field].astype(f32)
        cells = fc[field].astype(f32)
        for i in range(rows):
            g, u = i // group, i % group
            ends = [side[COLS * g : COLS * (g + 1)] for side in (left, right)]
            line = [
                pltpu.roll(ends[0], (COLS - REACH - REACH * u) % COLS, 0),
                cells[COLS * i : COLS * (i + 1)],
                pltpu.roll(ends[1], (COLS - REACH * u) % COLS, 0),
                zeros,
            ]
            ext[field, pl.ds((i + 1) * SLOTS, SLOTS)] = jnp.concatenate(line, 0).astype(bf16)

    def extend_ends(field):
        gathered = polar[field].astype(f32).reshape(n, 2, COLS, channels)
        pole_rows = [gathered[:, r].reshape(n * COLS, channels) for r in range(2)]
        zeros = jnp.zeros((COLS, channels), f32)
        turned = gathered[n // 2 - 1 : n // 2 + 2]
        turned = jnp.where(north, turned[:, 0], turned[:, 1])
        beside = below[field].astype(f32).reshape(3, 2, COLS, channels)
        beside = jnp.where(north, beside[:, 0], beside[:, 1])
        top = jnp.where(north, turned, beside).reshape(3 * COLS, channels)
        bottom = jnp.where(north, beside, turned).reshape(3 * COLS, channels)
        ext[field, pl.ds(0, SLOTS)] = jnp.concatenate([top, zeros], 0).astype(bf16)
        ext[field, pl.ds((rows + 1) * SLOTS, SLOTS)] = jnp.concatenate([bottom, zeros], 0).astype(bf16)
        return jnp.concatenate(pole_rows, 0).astype(bf16)

    flip = lax.broadcasted_iota(jnp.int32, (128, 128), 0) + lax.broadcasted_iota(
        jnp.int32, (128, 128), 1
    )
    flip = jnp.where(flip == 127, 1.0, 0.0).astype(bf16)
    flip_high, flip_low = split(h_ref[...])
    rev[...] = mul(flip_high, flip) + mul(flip_low, flip)
    for r in range(2):
        turned = [
            rev[pl.ds(lat * 4 + a * 2 + r, kernels, stride=8), :] for a in range(2)
        ]
        for j in range(COLS):
            for a in range(2):
                circ[a, pl.ds((r * COLS + j) * kernels, kernels)] = pltpu.roll(turned[a], j + 1, 1)
    def forward(p, polar_part=None):
        taps = [
            taps_f[kernels * (2 * p + x // COLS) : kernels * (2 * p + x // COLS + 1),
                   x * window : (x + 1) * window]
            for x in range(16)
        ]
        taps = jnp.concatenate(taps, 0).astype(bf16)
        value = mul(taps, ext[0, pl.ds(2 * p * SLOTS, window)])
        if p == 0:
            value = value + jnp.where(north, polar_part, 0.0)
        elif p == pairs - 1:
            value = value + jnp.where(north, 0.0, polar_part)
        for h in range(channels // 128):
            sums[h, pl.ds(16 * kernels * p, 16 * kernels)] = value[:, 128 * h : 128 * (h + 1)]

    for copy in field_copies[n - 1 :]:
        copy.wait()
    extend_inside(0)
    for p in range(1, pairs - 1):
        forward(p)
    for copy in field_copies[: n - 1]:
        copy.wait()
    cotangent_copies = send_field(1)
    cotangent_copies.append(push(rims, near, send_misc.at[0, 5], recv_misc.at[0, 5], (other, lon)))
    poles = extend_ends(0)
    polar_part = mul(high, poles) + mul(low, poles)
    forward(0, polar_part)
    forward(pairs - 1, polar_part)

    cot = fc[1]

    def gradient(k):
        cells = [sums[h, pl.ds(k, points, stride=kernels), :] for h in range(channels // 128)]
        return mul(jnp.concatenate(cells, 1).astype(bf16), cot, ((0,), (0,)))

    line, spot = lon // GROUP, lax.rem(lon, GROUP)

    def in_plane(t):
        return (lat, line * GROUP + lax.rem(spot + t, GROUP))

    def on_line(t):
        return (lat, lax.rem(line + t, lines) * GROUP + spot)

    def rows_of(line_at, spot_at):
        return pl.ds(pl.multiple_of((line_at * GROUP + spot_at) * chunk, chunk), chunk)

    order = list(range(1, lines)) + [0]
    to_sib = {}
    for t in order:
        j = lax.rem(line + t, lines)
        sib_out[t] = gradient(other * half_k + j).astype(bf16)
        to_sib[t] = push(sib_out.at[t], sib_in.at[t], send_sib.at[t], recv_sib.at[t], (other, lon))
    for t in order:
        own[t] = gradient(lat * half_k + lax.rem(line + t, lines))
    plane = {}
    for t in order:
        j = lax.rem(line + t, lines)
        to_sib[t].wait()
        part[pl.ds(pl.multiple_of(j * channels, channels), channels)] = (
            own[t] + sib_in[t].astype(f32)
        ).astype(bf16)
        plane[t] = [
            push(
                part.at[rows_of(j, lax.rem(spot + u, GROUP))], plane_terms.at[u, t],
                send_plane.at[u, t], recv_plane.at[u, t], in_plane(u),
            )
            for u in range(1, GROUP)
        ]
    taps_each = 3 * (2 * REACH + 1)
    step = 2 * (2 * REACH + 1)
    first_taps = lane < taps_each - step
    up = jnp.where(first_taps, by_row[0], 0.0)
    up = pltpu.roll(up, step, 1)
    down = pltpu.roll(by_row[-1], 128 - step, 1)
    down = jnp.where(first_taps, down, 0.0)
    cotangent_copies[-1].wait()
    beside = near[...]
    mat = jnp.concatenate(
        [jnp.where(north, up, beside)] + by_row + [jnp.where(north, beside, down)], 0
    )
    spread = mul(mat[:, :16].astype(bf16), d_ref[:, lanes:])
    part_of = lax.broadcasted_iota(jnp.int32, (kernels, window), 1) // SLOTS
    for p in range(pairs):
        for x in range(16):
            tile = jnp.zeros((kernels, window), f32)
            for q in range(4):
                i = kernels * (2 * p + q)
                tile = jnp.where(
                    part_of == q, spread[i : i + kernels, x * window : (x + 1) * window], tile
                )
            taps_b[pl.ds((16 * p + x) * kernels, kernels)] = tile
    along = {}
    for t in order:
        total = part[rows_of(lax.rem(line + t, lines), spot)].astype(f32)
        for u in range(1, GROUP):
            plane[t][u - 1].wait()
            total = total + plane_terms[u, t].astype(f32)
        if t:
            plane_sums[t] = total.astype(bf16)
            along[t] = push(
                plane_sums.at[t], line_terms.at[t], send_line.at[t], recv_line.at[t], on_line(t)
            )

    acc[...] = jnp.zeros_like(acc)
    for copy in cotangent_copies[:-1]:
        copy.wait()
    extend_inside(1)
    poles = extend_ends(1)
    loads[5].wait()

    def per_kernel(k, pole_acc):
        weight = w_ref[k]
        grad = mul(ext[1], weight, ((1,), (1,))).astype(bf16)
        for p in range(pairs):
            taps = taps_b[pl.ds(16 * kernels * p + k, 16, stride=kernels), :].astype(bf16)
            acc[pl.ds(16 * p, 16)] += mul(taps, grad[2 * p * SLOTS : 2 * p * SLOTS + window])
        pole_grad = mul(poles, weight, ((1,), (1,))).astype(bf16)
        high, low = split(
            jnp.concatenate([circ[a, pl.ds(k, 16, stride=kernels), :] for a in range(2)], 1)
        )
        return pole_acc + mul(high, pole_grad) + mul(low, pole_grad)

    pole_acc = jnp.zeros((16, channels), f32)
    pole_acc = lax.fori_loop(0, 1, per_kernel, pole_acc)
    here = rows_of(line, spot)
    for t in range(1, lines):
        along[t].wait()
        total = total + line_terms[t].astype(f32)
    mine[...] = total.astype(bf16)
    gw_ref[here] = mine[...]

    def spread_plane(src, at, t):
        return [
            push(src, gw_ref.at[at], send_copy.at[u, t], recv_copy.at[u, t], in_plane(u))
            for u in range(1, GROUP)
        ]

    near_first = sorted(range(1, lines), key=lambda t: min(t, lines - t))
    first = {
        t: push(mine, gw_ref.at[here], send_first.at[t], recv_first.at[t], on_line(t))
        for t in near_first
    }
    gather = spread_plane(mine, here, 0)
    done = 1
    for t in near_first:
        pole_acc = per_kernel(done, pole_acc)
        done += 1
        first[t].wait()
        at = rows_of(lax.rem(line - t + lines, lines), spot)
        gather += spread_plane(gw_ref.at[at], at, t)
    pole_acc = lax.fori_loop(done, kernels, per_kernel, pole_acc)
    acc[pl.ds(0, 16)] += jnp.where(north, pole_acc, 0.0)
    acc[pl.ds(points - 16, 16)] += jnp.where(north, 0.0, pole_acc)
    gf_ref[...] = acc[...].astype(bf16)
    for copy in gather:
        copy.wait()


def in_kernel(features, cotangent, weights, basis, polar_kernel, lon_reach):
    lat_rows, lon_cols, channels = features.shape
    kernels = weights.shape[0]
    n = lax.axis_size("lon")
    pairs, points = lat_rows // 2, lat_rows * lon_cols
    taps = 3 * (2 * REACH + 1)
    bf16, f32 = jnp.bfloat16, jnp.float32
    masked = basis.transpose(2, 3, 0, 1).reshape(taps * kernels, lat_rows)
    spread = jnp.asarray(spread_matrices(), bf16)
    half = kernels * channels // 2
    window, pack = 4 * SLOTS, lat_rows * REACH
    dma = pltpu.SemaphoreType.DMA
    vmem = pl.BlockSpec(memory_space=pltpu.VMEM)
    hbm = pl.BlockSpec(memory_space=pltpu.HBM)
    lines = n // GROUP
    grad_features, grad_weights = pl.pallas_call(
        functools.partial(fused, n),
        out_shape=(
            jax.ShapeDtypeStruct((points, channels), bf16),
            jax.ShapeDtypeStruct((half, channels), bf16),
        ),
        in_specs=[hbm] * 4 + [pl.BlockSpec(memory_space=pltpu.SMEM)] + [hbm] * 2,
        out_specs=(vmem, vmem),
        scratch_shapes=[
            pltpu.VMEM(weights.shape, bf16),
            pltpu.VMEM(masked.shape, bf16),
            pltpu.VMEM((kernels * 8, lon_cols * n), f32),
            pltpu.VMEM(spread.shape, bf16),
            dma((6,)),
            pltpu.VMEM((16 * kernels, 128), f32),
            pltpu.VMEM((kernels * lat_rows, 128), f32),
            pltpu.VMEM((2, points, channels), bf16),
            pltpu.VMEM((2, n, 16, channels), bf16),
            pltpu.VMEM((2, 2, pack, channels), bf16),
            pltpu.VMEM((2, 2, pack, channels), bf16),
            pltpu.VMEM((2, 3, 16, channels), bf16),
            pltpu.VMEM((kernels, 128), f32),
            pltpu.VMEM((kernels, 128), f32),
            pltpu.VMEM((lat_rows * kernels, 16 * window), f32),
            pltpu.VMEM((pairs * 16 * kernels, window), f32),
            pltpu.VMEM((kernels * 8, 128), f32),
            pltpu.VMEM((2, 16 * kernels, lon_cols * n), f32),
            pltpu.VMEM((2, (lat_rows + 2) * SLOTS, channels), bf16),
            pltpu.VMEM((channels // 128, points * kernels, 128), f32),
            pltpu.VMEM((lines, channels, channels), f32),
            pltpu.VMEM((lines, channels, channels), bf16),
            pltpu.VMEM((lines, channels, channels), bf16),
            pltpu.VMEM((half, channels), bf16),
            pltpu.VMEM((GROUP, lines, half // n, channels), bf16),
            pltpu.VMEM((lines, half // n, channels), bf16),
            pltpu.VMEM((lines, half // n, channels), bf16),
            pltpu.VMEM((half // n, channels), bf16),
            pltpu.VMEM((points, channels), f32),
            dma((2, n)), dma((2, n)), dma((2, 6)), dma((2, 6)), dma((4,)), dma((4,)),
            dma((GROUP, lines)), dma((GROUP, lines)), dma((lines,)), dma((lines,)),
            dma((GROUP, lines)), dma((GROUP, lines)), dma((lines,)), dma((lines,)),
        ],
        compiler_params=pltpu.CompilerParams(
            collective_id=0, has_side_effects=True, vmem_limit_bytes=56 * 2**20
        ),
    )(
        features.reshape(points, channels), cotangent.reshape(points, channels),
        weights, masked, lon_reach, polar_kernel.reshape(kernels * 8, lon_cols * n), spread,
    )
    return (
        grad_features.reshape(features.shape),
        grad_weights.astype(f32).reshape(kernels // 2, channels, channels),
    )


def choose(features, cotangent, weights, basis, polar_kernel, lon_reach):
    rows, cols, channels = features.shape
    n = lax.axis_size("lon")
    kernels = weights.shape[0]
    fits = (
        lax.axis_size("lat") == 2 and cols == COLS and n * COLS == 128 and n == GROUP * (kernels // 2) and rows % 8 == 0
        and kernels == 8 and (kernels // 2 * channels) % (16 * n) == 0
    )
    plan = in_kernel if fits else on_device
    return plan(features, cotangent, weights, basis, polar_kernel, lon_reach)


def solution(mesh):
    in_specs = (
        P("lat", "lon", None),
        P("lat", "lon", None),
        P(),
        P(None, "lat", None, None),
        P(),
        P("lat"),
    )
    out_specs = (P("lat", "lon", None), P("lat", None, None))
    return jax.shard_map(
        choose, mesh=mesh, in_specs=in_specs, out_specs=out_specs, check_vma=False
    )
```
